256 devices in a mesh: group: 16 (over x, z_lo), head: 16 (over y, z_hi, core).
Axes of the slice: x: 4, y: 4, z: 8 (z_hi: 2, z_lo: 4; z = z_hi * 4 + z_lo), core: 2. Of those that a mesh axis runs over, the one named last changes fastest.
Arguments:
- rows_in: bfloat16 [10240, 8192], P('group', 'head'), may hold values from -6 to 6
- w_query: bfloat16 [8192, 4096], P(None, 'head'), may hold values from -0.0625 to 0.0625
- w_key: bfloat16 [8192, 512], P(None, 'head'), may hold values from -0.0625 to 0.0625
- w_value: bfloat16 [8192, 512], P(None, 'head'), may hold values from -0.0625 to 0.0625
- w_out: bfloat16 [4096, 8192], P(None, 'head'), may hold values from -0.09375 to 0.09375
- kv_pool: bfloat16 [1024, 2, 512, 128], P('group', None, 'head'), may hold values from -256 to 256
- page_table: int32 [16, 32], replicated, may hold values from 0 to 1023, as said below
- image_pages: int32 [16, 4], P('group'), may hold values from 1 to 16, 32 in all within a row
- selected: int32 [16, 512], P('group'), may hold values from 0 to 4095, as said below
- text_len: int32 [16], P('group'), may hold values from 1 to 128, as said below
Outputs:
- output: bfloat16 [10240, 8192], P('group', 'head')
- new_pool: bfloat16 [1024, 2, 512, 128], P('group', None, 'head')
The draws below stay inside these ranges and needn't reach their ends.
Inputs may be any that keep to these rules, and one draw needn't show every extreme that they name: `page_table`: an entry is holder * 64 + page on that holder; no pool page is named twice in the whole table; in each group's row a quarter of the holders are named 4 times each, half of them 2 times each, the rest never. `selected`: each row holds 512 distinct positions in increasing order. `text_len`: some group has 128 live text tokens.
All inputs are finite; a program needn't handle non-finite values.
Results may differ from the reference program's by a relative error of at most 0.006.
The reference program's roundings to bfloat16 on the way (of `queries`, `key_new`, `kv_cache`, `full_kv`, `weights` and `attended`) count: a program that leaves them out, or rounds other values in their place, can miss the bound.
Values may be sent and summed in bfloat16 or wider, within the bound.
No kernel may reach another device: no remote copies, remote signals or barrier semaphores. Data moves between devices by JAX's collectives and lax.ppermute only.
A program may use at most 128 MiB of HBM per device.

```python
import math
import jax
import jax.numpy as jnp
import numpy as np
from jax import lax

D = 8192
H = 32
KVH = 4
HD = 128
PAGE = 128
IMGS = 4
CTXP = 32
TXT = 128
POOL_DEV = 64
MAXP = 16
SEL = 512
R = 640
N_GROUP = 16


def draw_kv_pool(key, part):
    key = jax.random.fold_in(key, 11)
    pool_shape = (N_GROUP * POOL_DEV, 2, KVH * HD, PAGE)
    base_key = jax.random.fold_in(key, 0)
    return jax.random.normal(base_key, pool_shape, jnp.float32).astype(jnp.bfloat16)


def draw_page_table(key, part):
    key = jax.random.fold_in(key, 5)
    capacity = 2 * CTXP // N_GROUP
    local_key, group_key = jax.random.split(key)
    local_order = jax.vmap(lambda holder_key: jax.random.permutation(holder_key, POOL_DEV))(jax.random.split(local_key, N_GROUP))

    def one_group(dest_key, dest_index):
        rank_key, order_key = jax.random.split(dest_key)
        holder_rank = jax.random.permutation(rank_key, N_GROUP)
        counts = jnp.where(holder_rank < N_GROUP // 4, capacity, jnp.where(holder_rank < 3 * N_GROUP // 4, capacity // 2, 0))
        image_ends = jnp.cumsum(counts)
        entry_index = jnp.arange(CTXP)
        owner_entry = jnp.sum(image_ends[None, :] <= entry_index[:, None], axis=1)
        shuffle = jax.random.permutation(order_key, CTXP)
        owners = owner_entry[shuffle]
        earlier = entry_index[None, :] < entry_index[:, None]
        slot_of = jnp.sum((owners[None, :] == owners[:, None]) & earlier, axis=1)
        local_page = local_order[owners, dest_index * capacity + slot_of]
        return owners * POOL_DEV + local_page
    return jax.vmap(one_group)(jax.random.split(group_key, N_GROUP), jnp.arange(N_GROUP)).astype(jnp.int32)


def draw_selected(key, part):
    key = jax.random.fold_in(key, 7)

    def one_group(group_key):
        position_order = jax.random.permutation(group_key, CTXP * PAGE)
        return jnp.sort(position_order[:SEL])
    return jax.vmap(one_group)(jax.random.split(key, N_GROUP)).astype(jnp.int32)


def draw_text_len(key, part):
    key = jax.random.fold_in(key, 9)
    first_key, second_key = jax.random.split(key)
    lengths = jax.random.randint(first_key, (N_GROUP,), 1, TXT + 1)
    longest = jax.random.randint(second_key, (), 0, N_GROUP)
    return jnp.where(jnp.arange(N_GROUP) == longest, TXT, lengths).astype(jnp.int32)


def steps_of(rng, shape, shards, low, high):
    gain, own = 1.0, jax.random.fold_in(rng, 6)
    for position, parts in shards:
        draws = jnp.exp(jax.random.uniform(jax.random.fold_in(own, position), (parts,), jnp.float32, low / len(shards), high / len(shards)))
        gain = gain * jnp.repeat(draws, shape[position] // parts).reshape([-1 if axis == position else 1 for axis in range(len(shape))])
    return gain


def profile(number_of, total, reach, skew):
    weights = [(1 << 20) // math.isqrt(standing ** skew) + 1 for standing in range(2, number_of + 1)]
    rest, given = total - reach - (number_of - 1), [1] * (number_of - 1)
    while rest > 0:
        movable = [i for i in range(number_of - 1) if given[i] < reach]
        whole, budget = sum([weights[i] for i in movable]), rest
        for i in movable:
            more = min(reach - given[i], max(1, budget * weights[i] // whole), rest)
            given[i] = given[i] + more
            rest = rest - more
    return np.array([reach] + given)


def ragged_sizes(own_key, number_of, total, limit, lean):
    if number_of == 2:
        one = jax.random.randint(own_key, (), max(1, total - limit), min(limit, total - 1) + 1)
        return jnp.stack([one, total - one])
    sizes = jnp.asarray(profile(number_of, total, limit, lean), jnp.int32)
    twos = (number_of - 1) // 2
    source_of, receiver = sizes[1:1 + 2 * twos:2], sizes[2:2 + 2 * twos:2]
    margin = jnp.minimum(source_of - 1, limit - receiver)
    passed = jax.random.randint(jax.random.fold_in(own_key, 1), (twos,), 0, 1 << 20) % (margin + 1)
    sizes = sizes.at[1:1 + 2 * twos:2].set(source_of - passed).at[2:2 + 2 * twos:2].set(receiver + passed)
    return sizes[jax.random.permutation(jax.random.fold_in(own_key, 2), number_of)]


def gaussian(stream_key, dims, scale, reach, cuts=(), kind=jnp.bfloat16):
    array = scale * jax.random.normal(stream_key, dims, jnp.float32)
    if cuts:
        array = array * steps_of(stream_key, dims, cuts, -0.22, 0.18)
    return jnp.clip(array, -reach, reach).astype(kind)


def setup_inputs(seed: int = 0) -> dict:
    key_of = jax.random.split(jax.random.key(seed), 11)
    rows_in = gaussian(key_of[0], (N_GROUP * R, D), 1.0, 6.0, ((0, 16), (1, 16)))
    w_query = gaussian(key_of[1], (D, H * HD), D ** -0.5, 0.0625, ((1, 16),))
    w_key = gaussian(key_of[2], (D, KVH * HD), D ** -0.5, 0.0625, ((1, 16),))
    w_value = gaussian(key_of[3], (D, KVH * HD), D ** -0.5, 0.0625, ((1, 16),))
    w_out = gaussian(key_of[4], (H * HD, D), (H * HD) ** -0.5, 0.09375, ((1, 16),))
    kv_pool = draw_kv_pool(jax.random.fold_in(key_of[10], 71), 0)
    page_table = draw_page_table(jax.random.fold_in(key_of[10], 71), 0)
    image_pages = jax.vmap(lambda own: ragged_sizes(own, IMGS, CTXP, MAXP, 1))(jax.random.split(key_of[7], N_GROUP)).reshape((N_GROUP, IMGS)).astype(jnp.int32)
    selected = draw_selected(jax.random.fold_in(key_of[10], 71), 0)
    text_len = draw_text_len(jax.random.fold_in(key_of[10], 71), 0)
    return dict(rows_in=rows_in, w_query=w_query, w_key=w_key, w_value=w_value, w_out=w_out, kv_pool=kv_pool, page_table=page_table, image_pages=image_pages, selected=selected, text_len=text_len)


def build_mask(chosen, counts, text_count):
    ctx_len = CTXP * PAGE
    image_ends = (jnp.cumsum(counts) * PAGE).astype(jnp.int32)
    positions = jnp.arange(ctx_len, dtype=jnp.int32)
    key_image = lax.optimization_barrier(jnp.sum(positions[:, None] >= image_ends[None, :], axis=1))
    query_image = lax.optimization_barrier(jnp.sum(chosen[:, None] >= image_ends[None, :], axis=1))
    image_rows = (key_image[None, :] == query_image[:, None]) & (positions[None, :] <= chosen[:, None])
    text_pos = jnp.arange(TXT, dtype=jnp.int32)
    text_rows = (text_pos[None, :] <= text_pos[:, None]) & (text_pos[None, :] < text_count)
    image_part = jnp.concatenate([image_rows, jnp.zeros((SEL, TXT), bool)], axis=1)
    text_part = jnp.concatenate([jnp.ones((TXT, ctx_len), bool), text_rows], axis=1)
    return jnp.concatenate([image_part, text_part], axis=0)

def reference(rows_in, w_query, w_key, w_value, w_out, kv_pool, page_table, image_pages, selected, text_len):
    score_scale = 1.0 / math.sqrt(HD)
    ctx_len = CTXP * PAGE
    kv_total = KVH * HD
    per_kv = H // KVH
    new_pool = kv_pool
    results = []
    for group_number in range(N_GROUP):
        group_rows = rows_in[group_number * R:(group_number + 1) * R]
        queries = jnp.dot(group_rows, w_query, preferred_element_type=jnp.float32).astype(jnp.bfloat16)
        key_new = jnp.dot(group_rows, w_key, preferred_element_type=jnp.float32).astype(jnp.bfloat16)
        value_new = jnp.dot(group_rows, w_value, preferred_element_type=jnp.float32).astype(jnp.bfloat16)
        page_row = page_table[group_number]
        fetched = kv_pool[page_row]
        kv_cache = jnp.transpose(fetched, (1, 2, 0, 3)).reshape(2, kv_total, ctx_len)
        refreshed = jnp.stack([key_new[:SEL].T, value_new[:SEL].T])
        kv_cache = kv_cache.at[:, :, selected[group_number]].set(refreshed)
        returned = jnp.transpose(kv_cache.reshape(2, kv_total, CTXP, PAGE), (2, 0, 1, 3))
        new_pool = new_pool.at[page_row].set(returned)
        text_kv = jnp.stack([key_new[SEL:].T, value_new[SEL:].T])
        full_kv = jnp.concatenate([kv_cache, text_kv], axis=2)
        allowed = build_mask(selected[group_number], image_pages[group_number], text_len[group_number])
        grouped_query = queries.astype(jnp.float32).reshape(R, KVH, per_kv, HD).transpose(1, 2, 0, 3)
        grouped_kv = full_kv.astype(jnp.float32).reshape(2, KVH, HD, -1)

        def one_head(operands):
            head_query, head_keys, head_values = operands
            scores = jnp.einsum('grd,ds->grs', head_query, head_keys) * score_scale
            scores = jnp.where(allowed[None], scores, -jnp.inf)
            row_peak = lax.optimization_barrier(jnp.max(scores, axis=2, keepdims=True))
            exponent_terms = jnp.exp(scores - row_peak)
            weights = (exponent_terms / lax.optimization_barrier(jnp.sum(exponent_terms, axis=2, keepdims=True))).astype(jnp.bfloat16)
            weights = lax.optimization_barrier(weights).astype(jnp.float32)
            return jnp.einsum('grs,ds->rgd', weights, head_values).astype(jnp.bfloat16)
        attended = lax.map(one_head, (grouped_query, grouped_kv[0], grouped_kv[1]))
        attended = attended.transpose(1, 0, 2, 3).reshape(R, H * HD)
        summed = jnp.dot(attended, w_out, preferred_element_type=jnp.float32)
        results.append(summed.astype(jnp.bfloat16))
    return (jnp.concatenate(results, axis=0), new_pool)
```

```python
import math

import jax
import jax.numpy as jnp
from jax import lax
from jax.experimental import pallas as pl
from jax.experimental.pallas import tpu as pltpu
from jax.sharding import PartitionSpec as P

H = 32
KVH = 4
HD = 128
PAGE = 128
CTXP = 32
TXT = 128
POOL_DEV = 64
SEL = 512
R = SEL + TXT
CTX = CTXP * PAGE
KEYS = 512
ROWS = 128
WINDOW = 256
EXP2_SCALE = math.log2(math.e) / math.sqrt(HD)
LOW = -1e30

CORE_SWAP = [(i, i ^ 1) for i in range(16)]
Z_SWAP = [(i, i ^ 2) for i in range(16)]
Y_UP = [(i, (i + 4) % 16) for i in range(16)]
Y_DOWN = [(i, (i - 4) % 16) for i in range(16)]


def swap_core(block):
    return lax.ppermute(block, "head", CORE_SWAP)


def swap_z(block):
    return lax.ppermute(block, "head", Z_SWAP)


def gather_y(block):
    half = block.shape[0] // 2
    below = lax.ppermute(block, "head", Y_UP)
    above = lax.ppermute(block, "head", Y_DOWN)
    far_top = lax.ppermute(below[:half], "head", Y_UP)
    far_bottom = lax.ppermute(above[half:], "head", Y_DOWN)
    far = jnp.concatenate([far_top, far_bottom], axis=0)
    return [(0, block), (3, below), (1, above), (2, far)]


def gathered_dot(block, weights, y, z_hi):
    far_plane = swap_z(block)
    parts = [(dy, 0, b) for dy, b in gather_y(block)]
    parts += [(dy, 1, b) for dy, b in gather_y(far_plane)]
    total = None
    for dy, dz, b in parts:
        which = lax.rem(y + dy, 4) * 2 + (z_hi ^ dz)
        part = jnp.dot(
            b,
            lax.dynamic_index_in_dim(weights, which, 0, keepdims=False),
            preferred_element_type=jnp.float32,
        )
        total = part if total is None else total + part
    return total


def attend_kernel(
    numbers, q, c0, c1, c2, c3, n0, n1, n2, n3, chosen, first, last, attended, returned, kv, fresh
):
    rank = numbers[40]
    text_count = numbers[41]
    for j, n in enumerate((n0, n1, n2, n3)):
        for c in range(2):
            place = pl.multiple_of(c * HD + (rank ^ j) * 32, 32)
            fresh[pl.ds(place, 32), :] = n[pl.ds(c * 32, 32), :]

    def page_step(k, carry):
        lanes = pl.ds(pl.multiple_of(k * PAGE, PAGE), PAGE)
        for j, piece in enumerate((c0, c1, c2, c3)):
            for c in range(2):
                place = pl.multiple_of(c * HD + (rank ^ j) * 32, 32)
                kv[pl.ds(place, 32), lanes] = piece[k, c]
        start = pl.multiple_of(numbers[k], PAGE)
        rows = pl.ds(start, WINDOW)
        slot = lax.broadcasted_iota(jnp.int32, (WINDOW, PAGE), 1) + k * PAGE
        hit = jnp.where(chosen[rows, :] == slot, 1.0, 0.0)
        found = jnp.max(hit, axis=0, keepdims=True)
        moved = jnp.dot(
            fresh[:, rows], hit.astype(jnp.bfloat16), preferred_element_type=jnp.float32
        )
        old = kv[:, lanes].astype(jnp.float32)
        kv[:, lanes] = jnp.where(found > 0.0, moved, old).astype(jnp.bfloat16)
        for c in range(2):
            place = pl.multiple_of(c * HD + rank * 32, 32)
            returned[k, c] = kv[pl.ds(place, 32), lanes]
        return carry

    lax.fori_loop(0, CTXP, page_step, 0)
    kv[:, pl.ds(CTX, TXT)] = fresh[:, pl.ds(SEL, TXT)]

    def fold(carry, scores, values):
        peak, total, mixed = carry
        new_peak = jnp.maximum(peak, jnp.max(scores, axis=1, keepdims=True))
        fade = jnp.exp2((peak - new_peak) * EXP2_SCALE)
        terms = jnp.exp2((scores - new_peak) * EXP2_SCALE)
        total = total * fade + jnp.sum(terms, axis=1, keepdims=True)
        mixed = mixed * fade + lax.dot_general(
            terms.astype(jnp.bfloat16),
            values,
            (((1,), (1,)), ((), ())),
            preferred_element_type=jnp.float32,
        )
        return new_peak, total, mixed

    for block in range(R // ROWS):
        rows = pl.ds(block * ROWS, ROWS)
        query = jnp.concatenate([q[rows, pl.ds(0, HD)], q[rows, pl.ds(HD, HD)]], axis=0)
        carry = (
            jnp.full((2 * ROWS, 1), LOW, jnp.float32),
            jnp.zeros((2 * ROWS, 1), jnp.float32),
            jnp.zeros((2 * ROWS, HD), jnp.float32),
        )
        image_rows = block < SEL // ROWS

        def key_step(k, carry, query=query, rows=rows, image_rows=image_rows):
            lanes = pl.ds(pl.multiple_of(k * KEYS, KEYS), KEYS)
            scores = jnp.dot(query, kv[pl.ds(0, HD), lanes], preferred_element_type=jnp.float32)
            if image_rows:
                slot = lax.broadcasted_iota(jnp.int32, (ROWS, KEYS), 1) + k * KEYS
                low = first[rows, pl.ds(0, 1)]
                high = last[rows, pl.ds(0, 1)]
                allowed = (slot >= low) & (slot <= high)
                scores = jnp.where(jnp.concatenate([allowed, allowed], axis=0), scores, LOW)
            return fold(carry, scores, kv[pl.ds(HD, HD), lanes])

        if image_rows:
            carry = lax.fori_loop(numbers[32 + block], numbers[36 + block], key_step, carry)
        else:
            carry = lax.fori_loop(0, CTX // KEYS, key_step, carry)
            lanes = pl.ds(CTX, TXT)
            scores = jnp.dot(query, kv[pl.ds(0, HD), lanes], preferred_element_type=jnp.float32)
            slot = lax.broadcasted_iota(jnp.int32, (TXT, TXT), 1)
            row = lax.broadcasted_iota(jnp.int32, (TXT, TXT), 0)
            allowed = (slot <= row) & (slot < text_count)
            scores = jnp.where(jnp.concatenate([allowed, allowed], axis=0), scores, LOW)
            carry = fold(carry, scores, kv[pl.ds(HD, HD), lanes])
        _, total, mixed = carry
        mixed = (mixed / total).astype(jnp.bfloat16)
        attended[rows, pl.ds(0, HD)] = mixed[:ROWS]
        attended[rows, pl.ds(HD, HD)] = mixed[ROWS:]


def attend(numbers, q, context, fresh, chosen, first, last):
    vmem = pl.BlockSpec(memory_space=pltpu.VMEM)
    return pl.pallas_call(
        attend_kernel,
        out_shape=(
            jax.ShapeDtypeStruct((R, 2 * HD), jnp.bfloat16),
            jax.ShapeDtypeStruct((CTXP, 2, 32, PAGE), jnp.bfloat16),
        ),
        in_specs=[pl.BlockSpec(memory_space=pltpu.SMEM)] + [vmem] * 12,
        out_specs=(vmem, vmem),
        scratch_shapes=[
            pltpu.VMEM((2 * HD, CTX + TXT), jnp.bfloat16),
            pltpu.VMEM((2 * HD, R), jnp.bfloat16),
        ],
        compiler_params=pltpu.CompilerParams(vmem_limit_bytes=32 * 1024 * 1024),
        cost_estimate=pl.CostEstimate(
            flops=4 * 10**9, bytes_accessed=8 * 10**6, transcendentals=5 * 10**6
        ),
        name="attend",
    )(numbers, q, *context, *fresh, chosen, first, last)


def slot_numbers(owners):
    entries = owners.shape[-1]
    earlier = jnp.arange(entries)[None, :] < jnp.arange(entries)[:, None]
    same_owner = owners[..., None, :] == owners[..., :, None]
    return jnp.sum(same_owner & earlier, axis=-1)


def body(
    rows_in, w_query, w_key, w_value, w_out, kv_pool, page_table, image_pages, selected, text_len
):
    group_count = lax.axis_size("group")
    group_index = lax.axis_index("group")
    head_index = lax.axis_index("head")
    core = head_index % 2
    z_hi = head_index // 2 % 2
    y = head_index // 4
    pool_pages = kv_pool.shape[0]
    capacity = 2 * CTXP // group_count

    def both_cores(weights, split):
        mine = lax.dynamic_index_in_dim(weights, core, 1, keepdims=False)
        theirs = swap_core(lax.dynamic_index_in_dim(weights, 1 - core, 1, keepdims=False))
        pieces = []
        for low, high in zip(split, split[1:]):
            pieces += [mine[:, :, low:high], theirs[:, :, low:high]]
        return jnp.concatenate(pieces, axis=2)

    w_in = jnp.concatenate([w_query, w_key, w_value], axis=1).reshape(8, 2, 512, 320)
    w_in = both_cores(w_in, (0, 256, 320))
    w_last = both_cores(w_out.reshape(8, 2, 256, 512), (0, 512))

    owners = page_table // POOL_DEV
    local_page = page_table % POOL_DEV
    slot_of = slot_numbers(owners)
    slot_range = jnp.arange(capacity)
    held_here = (owners == group_index)[:, :, None] & (
        slot_of[:, :, None] == slot_range[None, None, :]
    )
    send_valid = jnp.any(held_here, axis=1)
    send_index = jnp.sum(jnp.where(held_here, local_page[:, :, None], 0), axis=1)
    outgoing = jnp.where(
        send_valid[:, :, None, None, None], kv_pool[send_index], jnp.zeros((), kv_pool.dtype)
    )
    incoming = lax.all_to_all(outgoing, "group", split_axis=0, concat_axis=0, tiled=True)
    my_owners = lax.dynamic_index_in_dim(owners, group_index, 0, keepdims=False)
    my_slots = lax.dynamic_index_in_dim(slot_of, group_index, 0, keepdims=False)
    own_context = incoming[my_owners, my_slots]
    z_context = swap_z(own_context)
    context = [own_context, swap_core(own_context), z_context, swap_core(z_context)]

    sums = gathered_dot(rows_in, w_in, y, z_hi)
    arrived_sums = swap_core(jnp.concatenate([sums[:, 256:512], sums[:, 576:]], axis=1))
    queries = (sums[:, :256] + arrived_sums[:, :256]).astype(jnp.bfloat16)
    new_kv = (sums[:, 512:576] + arrived_sums[:, 256:]).astype(jnp.bfloat16).T
    z_kv = swap_z(new_kv)
    fresh = [new_kv, swap_core(new_kv), z_kv, swap_core(z_kv)]

    positions = selected[0]
    image_ends = jnp.cumsum(image_pages[0]) * PAGE
    image_first = jnp.max(
        jnp.where(positions[:, None] >= image_ends[None, :], image_ends[None, :], 0), axis=1
    )
    page_first = jnp.sum(positions[None, :] < (jnp.arange(CTXP) * PAGE)[:, None], axis=1)
    window = jnp.minimum(page_first // PAGE * PAGE, SEL - WINDOW)
    key_first = image_first[::ROWS] // KEYS
    key_end = positions[ROWS - 1 :: ROWS] // KEYS + 1
    numbers = jnp.concatenate(
        [window, key_first, key_end, (head_index % 4)[None], text_len]
    ).astype(jnp.int32)
    wide = lambda v: jnp.broadcast_to(v[:, None], (SEL, 128)).astype(jnp.int32)
    attended, returned = attend(
        numbers, queries, context, fresh, wide(positions), wide(image_first), wide(positions)
    )

    target = (my_owners[None, None, :] == jnp.arange(group_count)[:, None, None]) & (
        my_slots[None, None, :] == slot_range[None, :, None]
    )
    back_valid = jnp.any(target, axis=2)
    back_index = jnp.sum(jnp.where(target, jnp.arange(CTXP)[None, None, :], 0), axis=2)
    homeward = jnp.where(
        back_valid[:, :, None, None, None], returned[back_index], jnp.zeros((), returned.dtype)
    )
    arrived = lax.all_to_all(homeward, "group", split_axis=0, concat_axis=0, tiled=True)
    new_pool = kv_pool.at[jnp.where(send_valid, send_index, pool_pages)].set(arrived, mode="drop")

    out = gathered_dot(attended, w_last, y, z_hi)
    out = out[:, :512] + swap_core(out[:, 512:])
    return (out.astype(jnp.bfloat16), new_pool)


def solution(mesh):
    placed = (
        P("group", "head"),
        P(None, "head"),
        P(None, "head"),
        P(None, "head"),
        P(None, "head"),
        P("group", None, "head", None),
        P(),
        P("group", None),
        P("group", None),
        P("group"),
    )
    return jax.shard_map(
        body,
        mesh=mesh,
        in_specs=placed,
        out_specs=(P("group", "head"), P("group", None, "head", None)),
        check_vma=False,
    )
```

```python
import functools
import math

import jax
import jax.numpy as jnp
from jax import lax
from jax.experimental import pallas as pl
from jax.experimental.pallas import tpu as pltpu
from jax.sharding import PartitionSpec as P

H = 32
KVH = 4
HD = 128
PAGE = 128
CTXP = 32
TXT = 128
POOL_DEV = 64
SEL = 512
R = SEL + TXT
CTX = CTXP * PAGE
KEYS = 512
ROWS = 128
WINDOW = 256
EXP2_SCALE = math.log2(math.e) / math.sqrt(HD)
LOW = -1e30
VMEM_BYTES = 60 * 1024 * 1024
QUICK = pl.CostEstimate(flops=1000, bytes_accessed=1000, transcendentals=0)

CORE_SWAP = [(i, i ^ 1) for i in range(16)]
Z_SWAP = [(i, i ^ 2) for i in range(16)]
Y_LINES = [[4 * y + r for y in range(4)] for r in range(4)]
Y_UP = [(i, (i + 4) % 16) for i in range(16)]
Y_DOWN = [(i, (i - 4) % 16) for i in range(16)]
Y_FAR = [(i, (i + 8) % 16) for i in range(16)]


def swap_core(block):
    return lax.ppermute(block, "head", CORE_SWAP)


def swap_z(block):
    return lax.ppermute(block, "head", Z_SWAP)


def meet(*values):
    return lax.optimization_barrier(values)


def project_kernel(count, keys, start, end, order, *refs):
    refs = list(refs)
    take = lambda n: [refs.pop(0) for _ in range(n)]
    blocks = take(count)
    weights = take(3 if keys else 1)
    sums = [] if start else take(2 if keys else 1)
    results = take(2 if keys else 1)
    x, w = take(2)
    wkv = take(1)[0] if keys else None
    (sems,) = take(1)
    depth = x.shape[1] // count
    copies = []
    for i in range(count):
        rows = pl.ds(pl.multiple_of(order[i] * depth, depth), depth)
        here = pl.ds(i * depth, depth)
        copies.append(
            [
                pltpu.make_async_copy(weights[0].at[rows, :], w.at[here, :], sems.at[i, 0]),
                pltpu.make_async_copy(blocks[i], x.at[:, here], sems.at[i, 1]),
            ]
        )
        for c in range(2 if keys else 0):
            copies[i].append(
                pltpu.make_async_copy(
                    weights[1 + c].at[:, rows],
                    wkv.at[pl.ds(c * 32, 32), here],
                    sems.at[i, 2 + c],
                )
            )
        for copy in copies[i]:
            copy.start()
    totals = [None] * len(results) if start else [ref[...] for ref in sums]
    half = count // 2
    for i in range(0, count, half):
        for j in range(i, i + half):
            for copy in copies[j]:
                copy.wait()
        here = pl.ds(i * depth, half * depth)
        parts = [jnp.dot(x[:, here], w[here, :], preferred_element_type=jnp.float32)]
        if keys:
            parts.append(
                lax.dot_general(
                    x[:, here],
                    wkv[:, here],
                    (((1,), (1,)), ((), ())),
                    preferred_element_type=jnp.float32,
                )
            )
        totals = [p if t is None else t + p for t, p in zip(totals, parts)]
    if not end:
        for ref, total in zip(results, totals):
            ref[...] = total
        return
    results[0][...] = totals[0].astype(jnp.bfloat16)
    if keys:
        results[1][...] = totals[1].T.astype(jnp.bfloat16)


def project(pieces, weights, place, sums, end):
    y, z_hi, core = place
    order = [lax.rem(y + dy, 4) * 4 + (z_hi ^ dz) * 2 + (core ^ dc) for dy, dz, dc, _ in pieces]
    order = jnp.stack(order).astype(jnp.int32)
    blocks = [block for _, _, _, block in pieces]
    count = len(blocks)
    rows, depth = blocks[0].shape
    width = weights[0].shape[1]
    keys = len(weights) > 1
    vmem = pl.BlockSpec(memory_space=pltpu.VMEM)
    hbm = pl.BlockSpec(memory_space=pl.ANY)
    kind = jnp.bfloat16 if end else jnp.float32
    shapes = [jax.ShapeDtypeStruct((rows, width), kind)]
    if keys:
        shapes.append(jax.ShapeDtypeStruct((64, rows) if end else (rows, 64), kind))
    scratch = [
        pltpu.VMEM((rows, count * depth), jnp.bfloat16),
        pltpu.VMEM((count * depth, width), jnp.bfloat16),
    ]
    if keys:
        scratch.append(pltpu.VMEM((64, count * depth), jnp.bfloat16))
    scratch.append(pltpu.SemaphoreType.DMA((count, 4)))
    return pl.pallas_call(
        functools.partial(project_kernel, count, keys, sums is None, end),
        out_shape=shapes,
        in_specs=[pl.BlockSpec(memory_space=pltpu.SMEM)]
        + [hbm] * (len(blocks) + len(weights))
        + [vmem] * len(sums or []),
        out_specs=[vmem] * len(shapes),
        scratch_shapes=scratch,
        compiler_params=pltpu.CompilerParams(vmem_limit_bytes=VMEM_BYTES),
        cost_estimate=QUICK,
        name="project",
    )(order, *blocks, *weights, *(sums or []))


def along_y(block):
    return [lax.ppermute(block, "head", route) for route in (Y_UP, Y_DOWN, Y_FAR)]


def pieces(dz, dc, own, others):
    return [(0, dz, dc, own)] * (own is not None) + [
        (dy, dz, dc, b) for dy, b in zip((3, 1, 2), others)
    ]


def exchange(pages):
    return lax.all_to_all(pages, "group", 0, 0, tiled=True)


def mark_kernel(numbers, chosen, hits, found):
    def page_step(k, carry):
        rows = pl.ds(pl.multiple_of(numbers[k], PAGE), WINDOW)
        slot = lax.broadcasted_iota(jnp.int32, (WINDOW, PAGE), 1) + k * PAGE
        hit = jnp.where(chosen[rows, :] == slot, 1.0, 0.0)
        hits[k] = hit.astype(jnp.bfloat16)
        found[k] = jnp.broadcast_to(jnp.max(hit, axis=0, keepdims=True), (8, PAGE))
        return carry

    lax.fori_loop(0, CTXP, page_step, 0)


def mark(numbers, chosen):
    vmem = pl.BlockSpec(memory_space=pltpu.VMEM)
    return pl.pallas_call(
        mark_kernel,
        out_shape=(
            jax.ShapeDtypeStruct((CTXP, WINDOW, PAGE), jnp.bfloat16),
            jax.ShapeDtypeStruct((CTXP, 8, PAGE), jnp.float32),
        ),
        in_specs=[pl.BlockSpec(memory_space=pltpu.SMEM), vmem],
        out_specs=(vmem, vmem),
        compiler_params=pltpu.CompilerParams(vmem_limit_bytes=32 * 1024 * 1024),
        cost_estimate=QUICK,
        name="mark",
    )(numbers, chosen)


def refresh_kernel(count, numbers, *refs):
    context, new = refs[:count], refs[count : 2 * count]
    hits, found, result, fresh = refs[2 * count :]
    rank = numbers[40] if count > 1 else 0
    width = 32 * count
    places = [
        [pl.multiple_of(c * width + (rank ^ j) * 32, 32) for c in range(2)] for j in range(count)
    ]
    for j in range(count):
        for c in range(2):
            fresh[pl.ds(places[j][c], 32), :] = new[j][pl.ds(c * 32, 32), :]

    def page_step(k, carry):
        rows = pl.ds(pl.multiple_of(numbers[k], PAGE), WINDOW)
        moved = jnp.dot(fresh[:, rows], hits[k], preferred_element_type=jnp.float32)
        taken = found[k, pl.ds(0, 1), :] > 0.0
        if count == 1:
            old = context[0][k].reshape(2 * width, PAGE).astype(jnp.float32)
            now = jnp.where(taken, moved, old).astype(jnp.bfloat16)
            result[k] = now.reshape(2, width, PAGE)
            return carry
        lanes = pl.ds(pl.multiple_of(k * PAGE, PAGE), PAGE)
        for j in range(count):
            for c in range(2):
                result[pl.ds(places[j][c], 32), lanes] = context[j][k, c]
        old = result[:, lanes].astype(jnp.float32)
        result[:, lanes] = jnp.where(taken, moved, old).astype(jnp.bfloat16)
        return carry

    lax.fori_loop(0, CTXP, page_step, 0, unroll=4)
    if count > 1:
        result[:, pl.ds(CTX, TXT)] = fresh[:, pl.ds(SEL, TXT)]


def attend_kernel(numbers, q, kv, first, last, attended):
    text_count = numbers[41]

    def fold(carry, scores, values):
        peak, total, mixed = carry
        new_peak = jnp.maximum(peak, jnp.max(scores, axis=1, keepdims=True))
        fade = jnp.exp2((peak - new_peak) * EXP2_SCALE)
        terms = jnp.exp2((scores - new_peak) * EXP2_SCALE)
        total = total * fade + jnp.sum(terms, axis=1, keepdims=True)
        mixed = mixed * fade + lax.dot_general(
            terms.astype(jnp.bfloat16),
            values,
            (((1,), (1,)), ((), ())),
            preferred_element_type=jnp.float32,
        )
        return new_peak, total, mixed

    for block in range(R // ROWS):
        rows = pl.ds(block * ROWS, ROWS)
        query = jnp.concatenate([q[rows, pl.ds(0, HD)], q[rows, pl.ds(HD, HD)]], axis=0)
        carry = (
            jnp.full((2 * ROWS, 1), LOW, jnp.float32),
            jnp.zeros((2 * ROWS, 1), jnp.float32),
            jnp.zeros((2 * ROWS, HD), jnp.float32),
        )
        image_rows = block < SEL // ROWS

        def key_step(k, carry, query=query, rows=rows, image_rows=image_rows):
            lanes = pl.ds(pl.multiple_of(k * KEYS, KEYS), KEYS)
            scores = jnp.dot(query, kv[pl.ds(0, HD), lanes], preferred_element_type=jnp.float32)
            if image_rows:
                slot = lax.broadcasted_iota(jnp.int32, (ROWS, KEYS), 1) + k * KEYS
                low = first[rows, pl.ds(0, 1)]
                high = last[rows, pl.ds(0, 1)]
                allowed = (slot >= low) & (slot <= high)
                scores = jnp.where(jnp.concatenate([allowed, allowed], axis=0), scores, LOW)
            return fold(carry, scores, kv[pl.ds(HD, HD), lanes])

        if image_rows:
            carry = lax.fori_loop(numbers[32 + block], numbers[36 + block], key_step, carry)
        else:
            carry = lax.fori_loop(0, CTX // KEYS, key_step, carry)
            lanes = pl.ds(CTX, TXT)
            scores = jnp.dot(query, kv[pl.ds(0, HD), lanes], preferred_element_type=jnp.float32)
            slot = lax.broadcasted_iota(jnp.int32, (TXT, TXT), 1)
            row = lax.broadcasted_iota(jnp.int32, (TXT, TXT), 0)
            allowed = (slot <= row) & (slot < text_count)
            scores = jnp.where(jnp.concatenate([allowed, allowed], axis=0), scores, LOW)
            carry = fold(carry, scores, kv[pl.ds(HD, HD), lanes])
        _, total, mixed = carry
        mixed = (mixed / total).astype(jnp.bfloat16)
        attended[rows, pl.ds(0, HD)] = mixed[:ROWS]
        attended[rows, pl.ds(HD, HD)] = mixed[ROWS:]


def refresh(numbers, context, fresh, marks):
    vmem = pl.BlockSpec(memory_space=pltpu.VMEM)
    count = len(context)
    shape = (2 * HD, CTX + TXT) if count > 1 else (CTXP, 2, 32, PAGE)
    return pl.pallas_call(
        functools.partial(refresh_kernel, count),
        out_shape=jax.ShapeDtypeStruct(shape, jnp.bfloat16),
        in_specs=[pl.BlockSpec(memory_space=pltpu.SMEM)] + [vmem] * (2 * count + 2),
        out_specs=vmem,
        scratch_shapes=[pltpu.VMEM((64 * count, R), jnp.bfloat16)],
        compiler_params=pltpu.CompilerParams(vmem_limit_bytes=32 * 1024 * 1024),
        cost_estimate=QUICK,
        name="refresh",
    )(numbers, *context, *fresh, *marks)


def attend(numbers, q, kv, first, last):
    vmem = pl.BlockSpec(memory_space=pltpu.VMEM)
    return pl.pallas_call(
        attend_kernel,
        out_shape=jax.ShapeDtypeStruct((R, 2 * HD), jnp.bfloat16),
        in_specs=[pl.BlockSpec(memory_space=pltpu.SMEM)] + [vmem] * 4,
        out_specs=vmem,
        compiler_params=pltpu.CompilerParams(vmem_limit_bytes=32 * 1024 * 1024),
        cost_estimate=QUICK,
        name="attend",
    )(numbers, q, kv, first, last)


def replace_kernel(places, pool, pages, out):
    out[...] = pool[...]

    def step(i, carry):
        place = places[i]

        @pl.when(place < POOL_DEV)
        def _():
            out[jnp.minimum(place, POOL_DEV - 1)] = pages[i]

        return carry

    lax.fori_loop(0, places.shape[0], step, 0)


def replace(places, pool, pages):
    vmem = pl.BlockSpec(memory_space=pltpu.VMEM)
    return pl.pallas_call(
        replace_kernel,
        out_shape=jax.ShapeDtypeStruct(pool.shape, pool.dtype),
        in_specs=[pl.BlockSpec(memory_space=pltpu.SMEM), vmem, vmem],
        out_specs=vmem,
        compiler_params=pltpu.CompilerParams(vmem_limit_bytes=16 * 1024 * 1024),
        cost_estimate=QUICK,
        name="replace",
    )(places, pool, pages)


def slot_numbers(owners):
    entries = owners.shape[-1]
    earlier = jnp.arange(entries)[None, :] < jnp.arange(entries)[:, None]
    same_owner = owners[..., None, :] == owners[..., :, None]
    return jnp.sum(same_owner & earlier, axis=-1)


def body(
    rows_in, w_query, w_key, w_value, w_out, kv_pool, page_table, image_pages, selected, text_len
):
    group_index = lax.axis_index("group")
    head_index = lax.axis_index("head")
    place = (head_index // 4, head_index // 2 % 2, head_index % 2)
    capacity = 2 * CTXP // lax.axis_size("group")
    page_shape = kv_pool.shape[1:]

    far = swap_z(rows_in)
    near = along_y(rows_in)
    near_core, page_table = meet(swap_core(rows_in), page_table)

    owners = page_table // POOL_DEV
    local_page = page_table % POOL_DEV
    slot_of = slot_numbers(owners)
    held_here = (owners == group_index)[:, :, None] & (
        slot_of[:, :, None] == jnp.arange(capacity)[None, None, :]
    )
    held_place = jnp.sum(jnp.where(held_here, local_page[:, :, None], 0), axis=1)
    held_valid = jnp.any(held_here, axis=1)
    my_owners = lax.dynamic_index_in_dim(owners, group_index, 0, keepdims=False)
    my_slots = lax.dynamic_index_in_dim(slot_of, group_index, 0, keepdims=False)
    pages = kv_pool[held_place]
    near[0], near[1], far, pages = meet(near[0], near[1], far, pages)
    pages = exchange(pages)
    near_cores = [swap_core(b) for b in near]
    far, near_core, *near_cores = meet(far, near_core, *near_cores)

    far_core = swap_core(far)
    fars = along_y(far)
    weights = (w_query, w_key.T, w_value.T)
    blocks = pieces(0, 0, rows_in, near) + pieces(0, 1, near_core, near_cores)
    blocks += pieces(1, 0, far, []) + pieces(1, 1, far_core, [])
    sums = project(blocks, weights, place, None, False)
    positions = selected[0]
    image_ends = jnp.cumsum(image_pages[0]) * PAGE
    image_first = jnp.max(
        jnp.where(positions[:, None] >= image_ends[None, :], image_ends[None, :], 0), axis=1
    )
    page_first = jnp.sum(positions[None, :] < (jnp.arange(CTXP) * PAGE)[:, None], axis=1)
    window = jnp.minimum(page_first // PAGE * PAGE, SEL - WINDOW)
    key_first = image_first[::ROWS] // KEYS
    key_end = positions[ROWS - 1 :: ROWS] // KEYS + 1
    numbers = jnp.concatenate(
        [window, key_first, key_end, (head_index % 4)[None], text_len]
    ).astype(jnp.int32)
    wide = lambda v: jnp.broadcast_to(v[:, None], (SEL, 128)).astype(jnp.int32)
    wide_positions, wide_first = wide(positions), wide(image_first)
    target = (my_owners == jnp.arange(16)[:, None])[:, None, :] & (
        my_slots == jnp.arange(capacity)[:, None]
    )
    back_index = jnp.sum(jnp.where(target, jnp.arange(CTXP), 0), axis=2)
    marks = mark(numbers, wide_positions)

    values = meet(pages, *sums, *marks, numbers, wide_first, back_index, my_owners, my_slots)
    pages, sums, marks = values[0], values[1:3], values[3:5]
    numbers, wide_first, back_index, my_owners, my_slots = values[5:]
    own_context = pages[my_owners, my_slots]
    z_context = swap_z(own_context)
    core_context = swap_core(own_context)
    own_context, *fars = meet(own_context, *fars)
    far_cores = [swap_core(b) for b in fars]
    core_context, *sums = meet(core_context, *sums)
    blocks = pieces(1, 0, None, fars) + pieces(1, 1, None, far_cores)
    queries, new_kv = project(blocks, weights, place, sums, True)
    z_kv = swap_z(new_kv)
    core_kv = swap_core(new_kv)

    returned = refresh(numbers, [own_context], [new_kv], marks)
    homeward = returned[back_index]
    z_kv, core_kv, homeward, z_context = meet(z_kv, core_kv, homeward, z_context)
    arrived = exchange(homeward)

    context = [own_context, core_context, z_context, swap_core(z_context)]
    fresh = [new_kv, core_kv, z_kv, swap_core(z_kv)]
    kv = refresh(numbers, context, fresh, marks)
    attended = attend(numbers, queries, kv, wide_first, wide_positions)

    far = swap_z(attended)
    near = along_y(attended)
    near_core = swap_core(attended)
    near_cores = [swap_core(b) for b in near]
    far, near_core, *near_cores = meet(far, near_core, *near_cores)

    far_core = swap_core(far)
    fars = along_y(far)
    blocks = pieces(0, 0, attended, near) + pieces(0, 1, near_core, near_cores)
    blocks += pieces(1, 0, far, []) + pieces(1, 1, far_core, [])
    sums = project(blocks, (w_out,), place, None, False)
    values = meet(*fars, *sums)
    fars, sums = values[:3], values[3:]
    far_cores = [swap_core(b) for b in fars]
    places = jnp.where(held_valid, held_place, POOL_DEV).reshape(16 * capacity)
    new_pool = replace(
        places.astype(jnp.int32), kv_pool, arrived.reshape(16 * capacity, *page_shape)
    )
    new_pool, *far_cores = meet(new_pool, *far_cores)
    blocks = pieces(1, 0, None, fars) + pieces(1, 1, None, far_cores)
    (out,) = project(blocks, (w_out,), place, sums, True)
    return (out, new_pool)


def solution(mesh):
    placed = (
        P("group", "head"),
        P(None, "head"),
        P(None, "head"),
        P(None, "head"),
        P(None, "head"),
        P("group", None, "head", None),
        P(),
        P("group", None),
        P("group", None),
        P("group"),
    )
    return jax.shard_map(
        body,
        mesh=mesh,
        in_specs=placed,
        out_specs=(P("group", "head"), P("group", None, "head", None)),
        check_vma=False,
    )
```

```python
import functools
import math

import jax
import jax.numpy as jnp
from jax import lax
from jax.experimental import pallas as pl
from jax.experimental.pallas import tpu as pltpu
from jax.sharding import PartitionSpec as P

H = 32
KVH = 4
HD = 128
PAGE = 128
CTXP = 32
TXT = 128
POOL_DEV = 64
SEL = 512
R = SEL + TXT
CTX = CTXP * PAGE
KEYS = 1024
TEXT_KEYS = 2048
FIRST_PAGES = 8
ROWS = 128
WINDOW = 256
EXP2_SCALE = math.log2(math.e) / math.sqrt(HD)
LOW = -1e30
VMEM_BYTES = 60 * 1024 * 1024
QUICK = pl.CostEstimate(flops=1000, bytes_accessed=1000, transcendentals=0)

CORE_SWAP = [(i, i ^ 1) for i in range(16)]
Z_SWAP = [(i, i ^ 2) for i in range(16)]
Y_LINES = [[4 * y + r for y in range(4)] for r in range(4)]
Y_UP = [(i, (i + 4) % 16) for i in range(16)]
Y_DOWN = [(i, (i - 4) % 16) for i in range(16)]
Y_FAR = [(i, (i + 8) % 16) for i in range(16)]


def swap_core(block):
    return lax.ppermute(block, "head", CORE_SWAP)


def swap_z(block):
    return lax.ppermute(block, "head", Z_SWAP)


def meet(*values):
    return lax.optimization_barrier(values)


def project_kernel(count, keys, start, end, order, *refs):
    refs = list(refs)
    take = lambda n: [refs.pop(0) for _ in range(n)]
    blocks = take(count)
    weights = take(3 if keys else 1)
    sums = [] if start else take(2 if keys else 1)
    results = take(2 if keys else 1)
    x, w = take(2)
    wkv = take(1)[0] if keys else None
    (sems,) = take(1)
    depth = x.shape[1] // count
    copies = []
    for i in range(count):
        rows = pl.ds(pl.multiple_of(order[i] * depth, depth), depth)
        here = pl.ds(i * depth, depth)
        copies.append(
            [
                pltpu.make_async_copy(weights[0].at[rows, :], w.at[here, :], sems.at[i, 0]),
                pltpu.make_async_copy(blocks[i], x.at[:, here], sems.at[i, 1]),
            ]
        )
        for c in range(2 if keys else 0):
            copies[i].append(
                pltpu.make_async_copy(
                    weights[1 + c].at[:, rows],
                    wkv.at[pl.ds(c * 32, 32), here],
                    sems.at[i, 2 + c],
                )
            )
        for copy in copies[i]:
            copy.start()
    totals = [None] * len(results) if start else [ref[...] for ref in sums]
    half = count // 2
    for i in range(0, count, half):
        for j in range(i, i + half):
            for copy in copies[j]:
                copy.wait()
        here = pl.ds(i * depth, half * depth)
        parts = [jnp.dot(x[:, here], w[here, :], preferred_element_type=jnp.float32)]
        if keys:
            parts.append(
                lax.dot_general(
                    x[:, here],
                    wkv[:, here],
                    (((1,), (1,)), ((), ())),
                    preferred_element_type=jnp.float32,
                )
            )
        totals = [p if t is None else t + p for t, p in zip(totals, parts)]
    if not end:
        for ref, total in zip(results, totals):
            ref[...] = total
        return
    results[0][...] = totals[0].astype(jnp.bfloat16)
    if keys:
        results[1][...] = totals[1].T.astype(jnp.bfloat16)


def project(pieces, weights, place, sums, end):
    y, z_hi, core = place
    order = [lax.rem(y + dy, 4) * 4 + (z_hi ^ dz) * 2 + (core ^ dc) for dy, dz, dc, _ in pieces]
    order = jnp.stack(order).astype(jnp.int32)
    blocks = [block for _, _, _, block in pieces]
    count = len(blocks)
    rows, depth = blocks[0].shape
    width = weights[0].shape[1]
    keys = len(weights) > 1
    vmem = pl.BlockSpec(memory_space=pltpu.VMEM)
    hbm = pl.BlockSpec(memory_space=pl.ANY)
    kind = jnp.bfloat16 if end else jnp.float32
    shapes = [jax.ShapeDtypeStruct((rows, width), kind)]
    if keys:
        shapes.append(jax.ShapeDtypeStruct((64, rows) if end else (rows, 64), kind))
    scratch = [
        pltpu.VMEM((rows, count * depth), jnp.bfloat16),
        pltpu.VMEM((count * depth, width), jnp.bfloat16),
    ]
    if keys:
        scratch.append(pltpu.VMEM((64, count * depth), jnp.bfloat16))
    scratch.append(pltpu.SemaphoreType.DMA((count, 4)))
    return pl.pallas_call(
        functools.partial(project_kernel, count, keys, sums is None, end),
        out_shape=shapes,
        in_specs=[pl.BlockSpec(memory_space=pltpu.SMEM)]
        + [hbm] * (len(blocks) + len(weights))
        + [vmem] * len(sums or []),
        out_specs=[vmem] * len(shapes),
        scratch_shapes=scratch,
        compiler_params=pltpu.CompilerParams(vmem_limit_bytes=VMEM_BYTES),
        cost_estimate=QUICK,
        name="project",
    )(order, *blocks, *weights, *(sums or []))


def along_y(block):
    return [lax.ppermute(block, "head", route) for route in (Y_UP, Y_DOWN, Y_FAR)]


def pieces(dz, dc, own, others):
    return [(0, dz, dc, own)] * (own is not None) + [
        (dy, dz, dc, b) for dy, b in zip((3, 1, 2), others)
    ]


def exchange(pages):
    return lax.all_to_all(pages, "group", 0, 0, tiled=True)


def mark_kernel(numbers, chosen, hits, found):
    def page_step(k, carry):
        rows = pl.ds(pl.multiple_of(numbers[k], PAGE), WINDOW)
        slot = lax.broadcasted_iota(jnp.int32, (WINDOW, PAGE), 1) + k * PAGE
        hit = jnp.where(chosen[rows, :] == slot, 1.0, 0.0)
        hits[k] = hit.astype(jnp.bfloat16)
        found[k] = jnp.broadcast_to(jnp.max(hit, axis=0, keepdims=True), (8, PAGE))
        return carry

    lax.fori_loop(0, CTXP, page_step, 0)


def mark(numbers, chosen):
    vmem = pl.BlockSpec(memory_space=pltpu.VMEM)
    return pl.pallas_call(
        mark_kernel,
        out_shape=(
            jax.ShapeDtypeStruct((CTXP, WINDOW, PAGE), jnp.bfloat16),
            jax.ShapeDtypeStruct((CTXP, 8, PAGE), jnp.float32),
        ),
        in_specs=[pl.BlockSpec(memory_space=pltpu.SMEM), vmem],
        out_specs=(vmem, vmem),
        compiler_params=pltpu.CompilerParams(vmem_limit_bytes=32 * 1024 * 1024),
        cost_estimate=QUICK,
        name="mark",
    )(numbers, chosen)


def refresh_kernel(count, numbers, *refs):
    given = 6 if count > 1 else 1
    context, new = refs[:given], refs[given : given + count]
    hits, found, result, fresh = refs[given + count :]
    rank = numbers[40] if count > 1 else 0
    width = 32 * count
    places = [
        [pl.multiple_of(c * width + (rank ^ j) * 32, 32) for c in range(2)] for j in range(count)
    ]
    for j in range(count):
        for c in range(2):
            fresh[pl.ds(places[j][c], 32), :] = new[j][pl.ds(c * 32, 32), :]

    def page_step(k, carry, parts, before):
        rows = pl.ds(pl.multiple_of(numbers[k], PAGE), WINDOW)
        moved = jnp.dot(fresh[:, rows], hits[k], preferred_element_type=jnp.float32)
        taken = found[k, pl.ds(0, 1), :] > 0.0
        if count == 1:
            old = parts[0][k].reshape(2 * width, PAGE).astype(jnp.float32)
            now = jnp.where(taken, moved, old).astype(jnp.bfloat16)
            result[k] = now.reshape(2, width, PAGE)
            return carry
        lanes = pl.ds(pl.multiple_of(k * PAGE, PAGE), PAGE)
        for j in range(count):
            for c in range(2):
                page = k if j < 2 else k - before
                result[pl.ds(places[j][c], 32), lanes] = parts[j][page, c]
        old = result[:, lanes].astype(jnp.float32)
        result[:, lanes] = jnp.where(taken, moved, old).astype(jnp.bfloat16)
        return carry

    step = functools.partial(page_step, parts=context[:4], before=0)
    if count == 1:
        lax.fori_loop(0, CTXP, step, 0, unroll=4)
    else:
        lax.fori_loop(0, FIRST_PAGES, step, 0, unroll=4)
        step = functools.partial(
            page_step, parts=context[:2] + context[4:], before=FIRST_PAGES
        )
        lax.fori_loop(FIRST_PAGES, CTXP, step, 0, unroll=4)
        result[:, pl.ds(CTX, TXT)] = fresh[:, pl.ds(SEL, TXT)]


def attend_kernel(numbers, q, kv, first, last, attended):
    text_count = numbers[41]

    def fold(carry, scores, values):
        peak, total, mixed = carry
        new_peak = jnp.maximum(peak, jnp.max(scores, axis=1, keepdims=True))
        fade = jnp.exp2((peak - new_peak) * EXP2_SCALE)
        terms = jnp.exp2((scores - new_peak) * EXP2_SCALE)
        total = total * fade + jnp.sum(terms, axis=1, keepdims=True)
        mixed = mixed * fade + lax.dot_general(
            terms.astype(jnp.bfloat16),
            values,
            (((1,), (1,)), ((), ())),
            preferred_element_type=jnp.float32,
        )
        return new_peak, total, mixed

    for block in range(R // ROWS):
        rows = pl.ds(block * ROWS, ROWS)
        query = jnp.concatenate([q[rows, pl.ds(0, HD)], q[rows, pl.ds(HD, HD)]], axis=0)
        carry = (
            jnp.full((2 * ROWS, 1), LOW, jnp.float32),
            jnp.zeros((2 * ROWS, 1), jnp.float32),
            jnp.zeros((2 * ROWS, HD), jnp.float32),
        )
        image_rows = block < SEL // ROWS

        def image_step(k, carry, query=query, rows=rows, begin=numbers[32 + min(block, 3)]):
            wanted = begin + k * KEYS
            start = pl.multiple_of(jnp.minimum(wanted, CTX - KEYS), PAGE)
            lanes = pl.ds(start, KEYS)
            scores = jnp.dot(query, kv[pl.ds(0, HD), lanes], preferred_element_type=jnp.float32)
            slot = lax.broadcasted_iota(jnp.int32, (ROWS, KEYS), 1) + start
            low = jnp.maximum(first[rows, pl.ds(0, 1)], wanted)
            allowed = (slot >= low) & (slot <= last[rows, pl.ds(0, 1)])
            scores = jnp.where(jnp.concatenate([allowed, allowed], axis=0), scores, LOW)
            return fold(carry, scores, kv[pl.ds(HD, HD), lanes])

        if image_rows:
            carry = lax.fori_loop(0, numbers[36 + block], image_step, carry)
        else:
            for k in range(CTX // TEXT_KEYS):
                lanes = pl.ds(k * TEXT_KEYS, TEXT_KEYS)
                scores = jnp.dot(
                    query, kv[pl.ds(0, HD), lanes], preferred_element_type=jnp.float32
                )
                carry = fold(carry, scores, kv[pl.ds(HD, HD), lanes])
            lanes = pl.ds(CTX, TXT)
            scores = jnp.dot(query, kv[pl.ds(0, HD), lanes], preferred_element_type=jnp.float32)
            slot = lax.broadcasted_iota(jnp.int32, (TXT, TXT), 1)
            row = lax.broadcasted_iota(jnp.int32, (TXT, TXT), 0)
            allowed = (slot <= row) & (slot < text_count)
            scores = jnp.where(jnp.concatenate([allowed, allowed], axis=0), scores, LOW)
            carry = fold(carry, scores, kv[pl.ds(HD, HD), lanes])
        _, total, mixed = carry
        mixed = (mixed / total).astype(jnp.bfloat16)
        attended[rows, pl.ds(0, HD)] = mixed[:ROWS]
        attended[rows, pl.ds(HD, HD)] = mixed[ROWS:]


def refresh(numbers, context, fresh, marks):
    vmem = pl.BlockSpec(memory_space=pltpu.VMEM)
    count = len(fresh)
    shape = (2 * HD, CTX + TXT) if count > 1 else (CTXP, 2, 32, PAGE)
    return pl.pallas_call(
        functools.partial(refresh_kernel, count),
        out_shape=jax.ShapeDtypeStruct(shape, jnp.bfloat16),
        in_specs=[pl.BlockSpec(memory_space=pltpu.SMEM)] + [vmem] * (len(context) + count + 2),
        out_specs=vmem,
        scratch_shapes=[pltpu.VMEM((64 * count, R), jnp.bfloat16)],
        compiler_params=pltpu.CompilerParams(vmem_limit_bytes=32 * 1024 * 1024),
        cost_estimate=QUICK,
        name="refresh",
    )(numbers, *context, *fresh, *marks)


def attend(numbers, q, kv, first, last):
    vmem = pl.BlockSpec(memory_space=pltpu.VMEM)
    return pl.pallas_call(
        attend_kernel,
        out_shape=jax.ShapeDtypeStruct((R, 2 * HD), jnp.bfloat16),
        in_specs=[pl.BlockSpec(memory_space=pltpu.SMEM)] + [vmem] * 4,
        out_specs=vmem,
        compiler_params=pltpu.CompilerParams(vmem_limit_bytes=32 * 1024 * 1024),
        cost_estimate=QUICK,
        name="attend",
    )(numbers, q, kv, first, last)


def replace_kernel(places, pool, pages, out):
    out[...] = pool[...]

    def step(i, carry):
        place = places[i]

        @pl.when(place < POOL_DEV)
        def _():
            out[jnp.minimum(place, POOL_DEV - 1)] = pages[i]

        return carry

    lax.fori_loop(0, places.shape[0], step, 0)


def replace(places, pool, pages):
    vmem = pl.BlockSpec(memory_space=pltpu.VMEM)
    return pl.pallas_call(
        replace_kernel,
        out_shape=jax.ShapeDtypeStruct(pool.shape, pool.dtype),
        in_specs=[pl.BlockSpec(memory_space=pltpu.SMEM), vmem, vmem],
        out_specs=vmem,
        compiler_params=pltpu.CompilerParams(vmem_limit_bytes=16 * 1024 * 1024),
        cost_estimate=QUICK,
        name="replace",
    )(places, pool, pages)


def slot_numbers(owners):
    entries = owners.shape[-1]
    earlier = jnp.arange(entries)[None, :] < jnp.arange(entries)[:, None]
    same_owner = owners[..., None, :] == owners[..., :, None]
    return jnp.sum(same_owner & earlier, axis=-1)


def body(
    rows_in, w_query, w_key, w_value, w_out, kv_pool, page_table, image_pages, selected, text_len
):
    group_index = lax.axis_index("group")
    head_index = lax.axis_index("head")
    place = (head_index // 4, head_index // 2 % 2, head_index % 2)
    capacity = 2 * CTXP // lax.axis_size("group")
    page_shape = kv_pool.shape[1:]

    far = swap_z(rows_in)
    near = along_y(rows_in)
    near_core, page_table = meet(swap_core(rows_in), page_table)

    owners = page_table // POOL_DEV
    local_page = page_table % POOL_DEV
    slot_of = slot_numbers(owners)
    held_here = (owners == group_index)[:, :, None] & (
        slot_of[:, :, None] == jnp.arange(capacity)[None, None, :]
    )
    held_place = jnp.sum(jnp.where(held_here, local_page[:, :, None], 0), axis=1)
    held_valid = jnp.any(held_here, axis=1)
    my_owners = lax.dynamic_index_in_dim(owners, group_index, 0, keepdims=False)
    my_slots = lax.dynamic_index_in_dim(slot_of, group_index, 0, keepdims=False)
    pages = kv_pool[held_place]
    near[0], near[1], far, pages = meet(near[0], near[1], far, pages)
    pages = exchange(pages)
    near_cores = [swap_core(b) for b in near]
    far, near_core, *near_cores = meet(far, near_core, *near_cores)

    far_core = swap_core(far)
    fars = along_y(far)
    weights = (w_query, w_key.T, w_value.T)
    blocks = pieces(0, 0, rows_in, near) + pieces(0, 1, near_core, near_cores)
    blocks += pieces(1, 0, far, []) + pieces(1, 1, far_core, [])
    sums = project(blocks, weights, place, None, False)
    positions = selected[0]
    image_ends = jnp.cumsum(image_pages[0]) * PAGE
    image_first = jnp.max(
        jnp.where(positions[:, None] >= image_ends[None, :], image_ends[None, :], 0), axis=1
    )
    page_first = jnp.sum(positions[None, :] < (jnp.arange(CTXP) * PAGE)[:, None], axis=1)
    window = jnp.minimum(page_first // PAGE * PAGE, SEL - WINDOW)
    key_first = image_first[::ROWS]
    key_steps = (positions[ROWS - 1 :: ROWS] - key_first) // KEYS + 1
    numbers = jnp.concatenate(
        [window, key_first, key_steps, (head_index % 4)[None], text_len]
    ).astype(jnp.int32)
    wide = lambda v: jnp.broadcast_to(v[:, None], (SEL, 128)).astype(jnp.int32)
    wide_positions, wide_first = wide(positions), wide(image_first)
    target = (my_owners == jnp.arange(16)[:, None])[:, None, :] & (
        my_slots == jnp.arange(capacity)[:, None]
    )
    back_index = jnp.sum(jnp.where(target, jnp.arange(CTXP), 0), axis=2)
    marks = mark(numbers, wide_positions)

    values = meet(pages, *sums, *marks, numbers, wide_first, back_index, my_owners, my_slots)
    pages, sums, marks = values[0], values[1:3], values[3:5]
    numbers, wide_first, back_index, my_owners, my_slots = values[5:]
    own_context = pages[my_owners, my_slots]
    z_first = swap_z(own_context[:FIRST_PAGES])
    z_rest = swap_z(own_context[FIRST_PAGES:])
    core_context = swap_core(own_context)
    z_first, *fars = meet(z_first, *fars)
    far_cores = [swap_core(b) for b in fars]
    z_first_core = swap_core(z_first)
    core_context, *sums = meet(core_context, *sums)
    blocks = pieces(1, 0, None, fars) + pieces(1, 1, None, far_cores)
    queries, new_kv = project(blocks, weights, place, sums, True)
    z_kv = swap_z(new_kv)
    core_kv = swap_core(new_kv)

    returned = refresh(numbers, [own_context], [new_kv], marks)
    homeward = returned[back_index]
    z_kv, core_kv, homeward, z_rest = meet(z_kv, core_kv, homeward, z_rest)
    arrived = exchange(homeward)

    context = [own_context, core_context, z_first, z_first_core, z_rest, swap_core(z_rest)]
    fresh = [new_kv, core_kv, z_kv, swap_core(z_kv)]
    kv = refresh(numbers, context, fresh, marks)
    attended = attend(numbers, queries, kv, wide_first, wide_positions)

    far = swap_z(attended)
    near = along_y(attended)
    near_core = swap_core(attended)
    near_cores = [swap_core(b) for b in near]
    far, near_core, *near_cores = meet(far, near_core, *near_cores)

    far_core = swap_core(far)
    fars = along_y(far)
    blocks = pieces(0, 0, attended, near) + pieces(0, 1, near_core, near_cores)
    blocks += pieces(1, 0, far, []) + pieces(1, 1, far_core, [])
    sums = project(blocks, (w_out,), place, None, False)
    places = jnp.where(held_valid, held_place, POOL_DEV).reshape(16 * capacity)
    new_pool = replace(
        places.astype(jnp.int32), kv_pool, arrived.reshape(16 * capacity, *page_shape)
    )
    values = meet(*fars, new_pool, *sums)
    fars, new_pool, sums = values[:3], values[3], values[4:]
    far_cores = [swap_core(b) for b in fars]
    blocks = pieces(1, 0, None, fars) + pieces(1, 1, None, far_cores)
    (out,) = project(blocks, (w_out,), place, sums, True)
    return (out, new_pool)


def solution(mesh):
    placed = (
        P("group", "head"),
        P(None, "head"),
        P(None, "head"),
        P(None, "head"),
        P(None, "head"),
        P("group", None, "head", None),
        P(),
        P("group", None),
        P("group", None),
        P("group"),
    )
    return jax.shard_map(
        body,
        mesh=mesh,
        in_specs=placed,
        out_specs=(P("group", "head"), P("group", None, "head", None)),
        check_vma=False,
    )
```

```python
import functools
import math

import jax
import jax.numpy as jnp
from jax import lax
from jax.experimental import pallas as pl
from jax.experimental.pallas import tpu as pltpu
from jax.sharding import PartitionSpec as P

H = 32
KVH = 4
HD = 128
PAGE = 128
CTXP = 32
TXT = 128
POOL_DEV = 64
SEL = 512
R = SEL + TXT
CTX = CTXP * PAGE
KEYS = 1024
TEXT_KEYS = 2048
FIRST_PAGES = 8
ROWS = 128
WINDOW = 256
EXP2_SCALE = math.log2(math.e) / math.sqrt(HD)
LOW = -1e30
VMEM_BYTES = 60 * 1024 * 1024
QUICK = pl.CostEstimate(flops=1000, bytes_accessed=1000, transcendentals=0)

CORE_SWAP = [(i, i ^ 1) for i in range(16)]
Z_SWAP = [(i, i ^ 2) for i in range(16)]
Y_LINES = [[4 * y + r for y in range(4)] for r in range(4)]
Y_UP = [(i, (i + 4) % 16) for i in range(16)]
Y_DOWN = [(i, (i - 4) % 16) for i in range(16)]
Y_FAR = [(i, (i + 8) % 16) for i in range(16)]


def swap_core(block):
    return lax.ppermute(block, "head", CORE_SWAP)


def swap_z(block):
    return lax.ppermute(block, "head", Z_SWAP)


def meet(*values):
    return lax.optimization_barrier(values)


def project_kernel(count, keys, start, end, order, *refs):
    refs = list(refs)
    take = lambda n: [refs.pop(0) for _ in range(n)]
    blocks = take(count)
    weights = take(3 if keys else 1)
    sums = [] if start else take(2 if keys else 1)
    results = take(2 if keys else 1)
    x, w = take(2)
    wkv = take(1)[0] if keys else None
    (sems,) = take(1)
    depth = x.shape[1] // count
    copies = []
    for i in range(count):
        rows = pl.ds(pl.multiple_of(order[i] * depth, depth), depth)
        here = pl.ds(i * depth, depth)
        copies.append(
            [
                pltpu.make_async_copy(weights[0].at[rows, :], w.at[here, :], sems.at[i, 0]),
                pltpu.make_async_copy(blocks[i], x.at[:, here], sems.at[i, 1]),
            ]
        )
        for c in range(2 if keys else 0):
            copies[i].append(
                pltpu.make_async_copy(
                    weights[1 + c].at[:, rows],
                    wkv.at[pl.ds(c * 32, 32), here],
                    sems.at[i, 2 + c],
                )
            )
        for copy in copies[i]:
            copy.start()
    totals = [None] * len(results) if start else [ref[...] for ref in sums]
    half = count // 2
    for i in range(0, count, half):
        for j in range(i, i + half):
            for copy in copies[j]:
                copy.wait()
        here = pl.ds(i * depth, half * depth)
        parts = [jnp.dot(x[:, here], w[here, :], preferred_element_type=jnp.float32)]
        if keys:
            parts.append(
                lax.dot_general(
                    x[:, here],
                    wkv[:, here],
                    (((1,), (1,)), ((), ())),
                    preferred_element_type=jnp.float32,
                )
            )
        totals = [p if t is None else t + p for t, p in zip(totals, parts)]
    if not end:
        for ref, total in zip(results, totals):
            ref[...] = total
        return
    results[0][...] = totals[0].astype(jnp.bfloat16)
    if keys:
        results[1][...] = totals[1].T.astype(jnp.bfloat16)


def project(pieces, weights, place, sums, end):
    y, z_hi, core = place
    order = [lax.rem(y + dy, 4) * 4 + (z_hi ^ dz) * 2 + (core ^ dc) for dy, dz, dc, _ in pieces]
    order = jnp.stack(order).astype(jnp.int32)
    blocks = [block for _, _, _, block in pieces]
    count = len(blocks)
    rows, depth = blocks[0].shape
    width = weights[0].shape[1]
    keys = len(weights) > 1
    vmem = pl.BlockSpec(memory_space=pltpu.VMEM)
    hbm = pl.BlockSpec(memory_space=pl.ANY)
    kind = jnp.bfloat16 if end else jnp.float32
    shapes = [jax.ShapeDtypeStruct((rows, width), kind)]
    if keys:
        shapes.append(jax.ShapeDtypeStruct((64, rows) if end else (rows, 64), kind))
    scratch = [
        pltpu.VMEM((rows, count * depth), jnp.bfloat16),
        pltpu.VMEM((count * depth, width), jnp.bfloat16),
    ]
    if keys:
        scratch.append(pltpu.VMEM((64, count * depth), jnp.bfloat16))
    scratch.append(pltpu.SemaphoreType.DMA((count, 4)))
    return pl.pallas_call(
        functools.partial(project_kernel, count, keys, sums is None, end),
        out_shape=shapes,
        in_specs=[pl.BlockSpec(memory_space=pltpu.SMEM)]
        + [hbm] * (len(blocks) + len(weights))
        + [vmem] * len(sums or []),
        out_specs=[vmem] * len(shapes),
        scratch_shapes=scratch,
        compiler_params=pltpu.CompilerParams(vmem_limit_bytes=VMEM_BYTES),
        cost_estimate=QUICK,
        name="project",
    )(order, *blocks, *weights, *(sums or []))


def along_y(block):
    return [lax.ppermute(block, "head", route) for route in (Y_UP, Y_DOWN, Y_FAR)]


def pieces(dz, dc, own, others):
    return [(0, dz, dc, own)] * (own is not None) + [
        (dy, dz, dc, b) for dy, b in zip((3, 1, 2), others)
    ]


def exchange(pages):
    return lax.all_to_all(pages, "group", 0, 0, tiled=True)


def mark_kernel(numbers, chosen, hits, found):
    def page_step(k, carry):
        rows = pl.ds(pl.multiple_of(numbers[k], PAGE), WINDOW)
        slot = lax.broadcasted_iota(jnp.int32, (WINDOW, PAGE), 1) + k * PAGE
        hit = jnp.where(chosen[rows, :] == slot, 1.0, 0.0)
        hits[k] = hit.astype(jnp.bfloat16)
        found[k] = jnp.broadcast_to(jnp.max(hit, axis=0, keepdims=True), (8, PAGE))
        return carry

    lax.fori_loop(0, CTXP, page_step, 0)


def mark(numbers, chosen):
    vmem = pl.BlockSpec(memory_space=pltpu.VMEM)
    return pl.pallas_call(
        mark_kernel,
        out_shape=(
            jax.ShapeDtypeStruct((CTXP, WINDOW, PAGE), jnp.bfloat16),
            jax.ShapeDtypeStruct((CTXP, 8, PAGE), jnp.float32),
        ),
        in_specs=[pl.BlockSpec(memory_space=pltpu.SMEM), vmem],
        out_specs=(vmem, vmem),
        compiler_params=pltpu.CompilerParams(vmem_limit_bytes=32 * 1024 * 1024),
        cost_estimate=QUICK,
        name="mark",
    )(numbers, chosen)


def refresh_kernel(count, numbers, *refs):
    given = 6 if count > 1 else 1
    context, new = refs[:given], refs[given : given + count]
    hits, found, result, fresh = refs[given + count :]
    rank = numbers[40] if count > 1 else 0
    width = 32 * count
    places = [
        [pl.multiple_of(c * width + (rank ^ j) * 32, 32) for c in range(2)] for j in range(count)
    ]
    for j in range(count):
        for c in range(2):
            fresh[pl.ds(places[j][c], 32), :] = new[j][pl.ds(c * 32, 32), :]

    def page_step(k, carry, parts, before):
        rows = pl.ds(pl.multiple_of(numbers[k], PAGE), WINDOW)
        moved = jnp.dot(fresh[:, rows], hits[k], preferred_element_type=jnp.float32)
        taken = found[k, pl.ds(0, 1), :] > 0.0
        if count == 1:
            old = parts[0][k].reshape(2 * width, PAGE).astype(jnp.float32)
            now = jnp.where(taken, moved, old).astype(jnp.bfloat16)
            result[k] = now.reshape(2, width, PAGE)
            return carry
        lanes = pl.ds(pl.multiple_of(k * PAGE, PAGE), PAGE)
        for j in range(count):
            for c in range(2):
                page = k if j < 2 else k - before
                result[pl.ds(places[j][c], 32), lanes] = parts[j][page, c]
        old = result[:, lanes].astype(jnp.float32)
        result[:, lanes] = jnp.where(taken, moved, old).astype(jnp.bfloat16)
        return carry

    step = functools.partial(page_step, parts=context[:4], before=0)
    if count == 1:
        lax.fori_loop(0, CTXP, step, 0, unroll=4)
    else:
        lax.fori_loop(0, FIRST_PAGES, step, 0, unroll=4)
        step = functools.partial(
            page_step, parts=context[:2] + context[4:], before=FIRST_PAGES
        )
        lax.fori_loop(FIRST_PAGES, CTXP, step, 0, unroll=4)
        result[:, pl.ds(CTX, TXT)] = fresh[:, pl.ds(SEL, TXT)]


def attend_kernel(numbers, q, kv, first, last, attended):
    text_count = numbers[41]

    def fold(carry, scores, values):
        peak, total, mixed = carry
        new_peak = jnp.maximum(peak, jnp.max(scores, axis=1, keepdims=True))
        fade = jnp.exp2((peak - new_peak) * EXP2_SCALE)
        terms = jnp.exp2((scores - new_peak) * EXP2_SCALE)
        total = total * fade + jnp.sum(terms, axis=1, keepdims=True)
        mixed = mixed * fade + lax.dot_general(
            terms.astype(jnp.bfloat16),
            values,
            (((1,), (1,)), ((), ())),
            preferred_element_type=jnp.float32,
        )
        return new_peak, total, mixed

    for block in range(R // ROWS):
        rows = pl.ds(block * ROWS, ROWS)
        query = jnp.concatenate([q[rows, pl.ds(0, HD)], q[rows, pl.ds(HD, HD)]], axis=0)
        carry = (
            jnp.full((2 * ROWS, 1), LOW, jnp.float32),
            jnp.zeros((2 * ROWS, 1), jnp.float32),
            jnp.zeros((2 * ROWS, HD), jnp.float32),
        )
        image_rows = block < SEL // ROWS

        def image_step(k, carry, query=query, rows=rows, begin=numbers[32 + min(block, 3)]):
            wanted = begin + k * KEYS
            start = pl.multiple_of(jnp.minimum(wanted, CTX - KEYS), PAGE)
            lanes = pl.ds(start, KEYS)
            scores = jnp.dot(query, kv[pl.ds(0, HD), lanes], preferred_element_type=jnp.float32)
            slot = lax.broadcasted_iota(jnp.int32, (ROWS, KEYS), 1) + start
            low = jnp.maximum(first[rows, pl.ds(0, 1)], wanted)
            allowed = (slot >= low) & (slot <= last[rows, pl.ds(0, 1)])
            scores = jnp.where(jnp.concatenate([allowed, allowed], axis=0), scores, LOW)
            return fold(carry, scores, kv[pl.ds(HD, HD), lanes])

        if image_rows:
            carry = lax.fori_loop(0, numbers[36 + block], image_step, carry)
        else:
            for k in range(CTX // TEXT_KEYS):
                lanes = pl.ds(k * TEXT_KEYS, TEXT_KEYS)
                scores = jnp.dot(
                    query, kv[pl.ds(0, HD), lanes], preferred_element_type=jnp.float32
                )
                carry = fold(carry, scores, kv[pl.ds(HD, HD), lanes])
            lanes = pl.ds(CTX, TXT)
            scores = jnp.dot(query, kv[pl.ds(0, HD), lanes], preferred_element_type=jnp.float32)
            slot = lax.broadcasted_iota(jnp.int32, (TXT, TXT), 1)
            row = lax.broadcasted_iota(jnp.int32, (TXT, TXT), 0)
            allowed = (slot <= row) & (slot < text_count)
            scores = jnp.where(jnp.concatenate([allowed, allowed], axis=0), scores, LOW)
            carry = fold(carry, scores, kv[pl.ds(HD, HD), lanes])
        _, total, mixed = carry
        mixed = (mixed / total).astype(jnp.bfloat16)
        attended[rows, pl.ds(0, HD)] = mixed[:ROWS]
        attended[rows, pl.ds(HD, HD)] = mixed[ROWS:]


def refresh(numbers, context, fresh, marks):
    vmem = pl.BlockSpec(memory_space=pltpu.VMEM)
    count = len(fresh)
    shape = (2 * HD, CTX + TXT) if count > 1 else (CTXP, 2, 32, PAGE)
    return pl.pallas_call(
        functools.partial(refresh_kernel, count),
        out_shape=jax.ShapeDtypeStruct(shape, jnp.bfloat16),
        in_specs=[pl.BlockSpec(memory_space=pltpu.SMEM)] + [vmem] * (len(context) + count + 2),
        out_specs=vmem,
        scratch_shapes=[pltpu.VMEM((64 * count, R), jnp.bfloat16)],
        compiler_params=pltpu.CompilerParams(vmem_limit_bytes=32 * 1024 * 1024),
        cost_estimate=QUICK,
        name="refresh",
    )(numbers, *context, *fresh, *marks)


def attend(numbers, q, kv, first, last):
    vmem = pl.BlockSpec(memory_space=pltpu.VMEM)
    return pl.pallas_call(
        attend_kernel,
        out_shape=jax.ShapeDtypeStruct((R, 2 * HD), jnp.bfloat16),
        in_specs=[pl.BlockSpec(memory_space=pltpu.SMEM)] + [vmem] * 4,
        out_specs=vmem,
        compiler_params=pltpu.CompilerParams(vmem_limit_bytes=32 * 1024 * 1024),
        cost_estimate=QUICK,
        name="attend",
    )(numbers, q, kv, first, last)


def replace_kernel(places, pool, pages, out):
    out[...] = pool[...]

    def step(i, carry):
        place = places[i]

        @pl.when(place < POOL_DEV)
        def _():
            out[jnp.minimum(place, POOL_DEV - 1)] = pages[i]

        return carry

    lax.fori_loop(0, places.shape[0], step, 0)


def replace(places, pool, pages):
    vmem = pl.BlockSpec(memory_space=pltpu.VMEM)
    return pl.pallas_call(
        replace_kernel,
        out_shape=jax.ShapeDtypeStruct(pool.shape, pool.dtype),
        in_specs=[pl.BlockSpec(memory_space=pltpu.SMEM), vmem, vmem],
        out_specs=vmem,
        compiler_params=pltpu.CompilerParams(vmem_limit_bytes=16 * 1024 * 1024),
        cost_estimate=QUICK,
        name="replace",
    )(places, pool, pages)


def slot_numbers(owners):
    entries = owners.shape[-1]
    earlier = jnp.arange(entries)[None, :] < jnp.arange(entries)[:, None]
    same_owner = owners[..., None, :] == owners[..., :, None]
    return jnp.sum(same_owner & earlier, axis=-1)


def body(
    rows_in, w_query, w_key, w_value, w_out, kv_pool, page_table, image_pages, selected, text_len
):
    group_index = lax.axis_index("group")
    head_index = lax.axis_index("head")
    place = (head_index // 4, head_index // 2 % 2, head_index % 2)
    capacity = 2 * CTXP // lax.axis_size("group")
    page_shape = kv_pool.shape[1:]

    far = swap_z(rows_in)
    near = along_y(rows_in)
    near_core, page_table = meet(swap_core(rows_in), page_table)

    owners = page_table // POOL_DEV
    local_page = page_table % POOL_DEV
    slot_of = slot_numbers(owners)
    held_here = (owners == group_index)[:, :, None] & (
        slot_of[:, :, None] == jnp.arange(capacity)[None, None, :]
    )
    held_place = jnp.sum(jnp.where(held_here, local_page[:, :, None], 0), axis=1)
    held_valid = jnp.any(held_here, axis=1)
    my_owners = lax.dynamic_index_in_dim(owners, group_index, 0, keepdims=False)
    my_slots = lax.dynamic_index_in_dim(slot_of, group_index, 0, keepdims=False)
    pages = kv_pool[held_place]
    near[0], near[1], far, pages = meet(near[0], near[1], far, pages)
    pages = exchange(pages)
    near_cores = [swap_core(b) for b in near]
    far, near_core, *near_cores = meet(far, near_core, *near_cores)

    far_core = swap_core(far)
    fars = along_y(far)
    weights = (w_query, w_key.T, w_value.T)
    blocks = pieces(0, 0, rows_in, near) + pieces(0, 1, near_core, near_cores)
    blocks += pieces(1, 0, far, []) + pieces(1, 1, far_core, [])
    sums = project(blocks, weights, place, None, False)
    positions = selected[0]
    image_ends = jnp.cumsum(image_pages[0]) * PAGE
    image_first = jnp.max(
        jnp.where(positions[:, None] >= image_ends[None, :], image_ends[None, :], 0), axis=1
    )
    page_first = jnp.sum(positions[None, :] < (jnp.arange(CTXP) * PAGE)[:, None], axis=1)
    window = jnp.minimum(page_first // PAGE * PAGE, SEL - WINDOW)
    key_first = image_first[::ROWS]
    key_steps = (positions[ROWS - 1 :: ROWS] - key_first) // KEYS + 1
    numbers = jnp.concatenate(
        [window, key_first, key_steps, (head_index % 4)[None], text_len]
    ).astype(jnp.int32)
    wide = lambda v: jnp.broadcast_to(v[:, None], (SEL, 128)).astype(jnp.int32)
    wide_positions, wide_first = wide(positions), wide(image_first)
    target = (my_owners == jnp.arange(16)[:, None])[:, None, :] & (
        my_slots == jnp.arange(capacity)[:, None]
    )
    back_index = jnp.sum(jnp.where(target, jnp.arange(CTXP), 0), axis=2)
    marks = mark(numbers, wide_positions)

    values = meet(pages, *sums, *marks, numbers, wide_first, back_index, my_owners, my_slots)
    pages, sums, marks = values[0], values[1:3], values[3:5]
    numbers, wide_first, back_index, my_owners, my_slots = values[5:]
    own_context = pages[my_owners, my_slots]
    z_first = swap_z(own_context[:FIRST_PAGES])
    z_rest = swap_z(own_context[FIRST_PAGES:])
    core_context = swap_core(own_context)
    z_first, *fars = meet(z_first, *fars)
    far_cores = [swap_core(b) for b in fars]
    z_first_core = swap_core(z_first)
    core_context, *sums = meet(core_context, *sums)
    blocks = pieces(1, 0, None, fars) + pieces(1, 1, None, far_cores)
    queries, new_kv = project(blocks, weights, place, sums, True)
    z_kv = swap_z(new_kv)
    core_kv = swap_core(new_kv)

    returned = refresh(numbers, [own_context], [new_kv], marks)
    homeward = returned[back_index]
    z_kv, core_kv, homeward, z_rest = meet(z_kv, core_kv, homeward, z_rest)
    arrived = exchange(homeward)

    context = [own_context, core_context, z_first, z_first_core, z_rest, swap_core(z_rest)]
    fresh = [new_kv, core_kv, z_kv, swap_core(z_kv)]
    kv = refresh(numbers, context, fresh, marks)
    attended = attend(numbers, queries, kv, wide_first, wide_positions)

    far = swap_z(attended)
    near_core = swap_core(attended)
    attended, near_core = meet(attended, near_core)
    near = along_y(attended)
    near_cores = [swap_core(b) for b in near]

    far_core = swap_core(far)
    far, far_core, near_cores[0], near_cores[1] = meet(far, far_core, *near_cores[:2])
    fars = along_y(far)
    blocks = pieces(0, 0, attended, near) + pieces(0, 1, near_core, near_cores)
    blocks += pieces(1, 0, far, []) + pieces(1, 1, far_core, [])
    sums = project(blocks, (w_out,), place, None, False)
    places = jnp.where(held_valid, held_place, POOL_DEV).reshape(16 * capacity)
    new_pool = replace(
        places.astype(jnp.int32), kv_pool, arrived.reshape(16 * capacity, *page_shape)
    )
    values = meet(*fars, new_pool, *sums)
    fars, new_pool, sums = values[:3], values[3], values[4:]
    far_cores = [swap_core(b) for b in fars]
    blocks = pieces(1, 0, None, fars) + pieces(1, 1, None, far_cores)
    (out,) = project(blocks, (w_out,), place, sums, True)
    return (out, new_pool)


def solution(mesh):
    placed = (
        P("group", "head"),
        P(None, "head"),
        P(None, "head"),
        P(None, "head"),
        P(None, "head"),
        P("group", None, "head", None),
        P(),
        P("group", None),
        P("group", None),
        P("group"),
    )
    return jax.shard_map(
        body,
        mesh=mesh,
        in_specs=placed,
        out_specs=(P("group", "head"), P("group", None, "head", None)),
        check_vma=False,
    )
```

```python
import functools
import math

import jax
import jax.numpy as jnp
from jax import lax
from jax.experimental import pallas as pl
from jax.experimental.pallas import tpu as pltpu
from jax.sharding import PartitionSpec as P

H = 32
KVH = 4
HD = 128
PAGE = 128
CTXP = 32
TXT = 128
POOL_DEV = 64
SEL = 512
R = SEL + TXT
CTX = CTXP * PAGE
KEYS = 1024
TEXT_KEYS = 4096
FIRST_PAGES = 12
ROWS = 128
WINDOW = 256
EXP2_SCALE = math.log2(math.e) / math.sqrt(HD)
LOW = -1e30
VMEM_BYTES = 60 * 1024 * 1024
QUICK = pl.CostEstimate(flops=1000, bytes_accessed=1000, transcendentals=0)

CORE_SWAP = [(i, i ^ 1) for i in range(16)]
Z_SWAP = [(i, i ^ 2) for i in range(16)]
Y_LINES = [[4 * y + r for y in range(4)] for r in range(4)]
Y_UP = [(i, (i + 4) % 16) for i in range(16)]
Y_DOWN = [(i, (i - 4) % 16) for i in range(16)]
Y_FAR = [(i, (i + 8) % 16) for i in range(16)]


def swap_core(block):
    return lax.ppermute(block, "head", CORE_SWAP)


def swap_z(block):
    return lax.ppermute(block, "head", Z_SWAP)


def meet(*values):
    return lax.optimization_barrier(values)


def project_kernel(count, keys, start, end, order, *refs):
    refs = list(refs)
    take = lambda n: [refs.pop(0) for _ in range(n)]
    blocks = take(count)
    weights = take(3 if keys else 1)
    sums = [] if start else take(2 if keys else 1)
    results = take(2 if keys else 1)
    x, w = take(2)
    wkv = take(1)[0] if keys else None
    (sems,) = take(1)
    depth = x.shape[1] // count
    copies = []
    for i in range(count):
        rows = pl.ds(pl.multiple_of(order[i] * depth, depth), depth)
        here = pl.ds(i * depth, depth)
        copies.append(
            [
                pltpu.make_async_copy(weights[0].at[rows, :], w.at[here, :], sems.at[i, 0]),
                pltpu.make_async_copy(blocks[i], x.at[:, here], sems.at[i, 1]),
            ]
        )
        for c in range(2 if keys else 0):
            copies[i].append(
                pltpu.make_async_copy(
                    weights[1 + c].at[:, rows],
                    wkv.at[pl.ds(c * 32, 32), here],
                    sems.at[i, 2 + c],
                )
            )
        for copy in copies[i]:
            copy.start()
    totals = [None] * len(results) if start else [ref[...] for ref in sums]
    half = count // 2
    for i in range(0, count, half):
        for j in range(i, i + half):
            for copy in copies[j]:
                copy.wait()
        here = pl.ds(i * depth, half * depth)
        parts = [jnp.dot(x[:, here], w[here, :], preferred_element_type=jnp.float32)]
        if keys:
            parts.append(
                lax.dot_general(
                    x[:, here],
                    wkv[:, here],
                    (((1,), (1,)), ((), ())),
                    preferred_element_type=jnp.float32,
                )
            )
        totals = [p if t is None else t + p for t, p in zip(totals, parts)]
    if not end:
        for ref, total in zip(results, totals):
            ref[...] = total
        return
    results[0][...] = totals[0].astype(jnp.bfloat16)
    if keys:
        results[1][...] = totals[1].T.astype(jnp.bfloat16)


def project(pieces, weights, place, sums, end):
    y, z_hi, core = place
    order = [lax.rem(y + dy, 4) * 4 + (z_hi ^ dz) * 2 + (core ^ dc) for dy, dz, dc, _ in pieces]
    order = jnp.stack(order).astype(jnp.int32)
    blocks = [block for _, _, _, block in pieces]
    count = len(blocks)
    rows, depth = blocks[0].shape
    width = weights[0].shape[1]
    keys = len(weights) > 1
    vmem = pl.BlockSpec(memory_space=pltpu.VMEM)
    hbm = pl.BlockSpec(memory_space=pl.ANY)
    kind = jnp.bfloat16 if end else jnp.float32
    shapes = [jax.ShapeDtypeStruct((rows, width), kind)]
    if keys:
        shapes.append(jax.ShapeDtypeStruct((64, rows) if end else (rows, 64), kind))
    scratch = [
        pltpu.VMEM((rows, count * depth), jnp.bfloat16),
        pltpu.VMEM((count * depth, width), jnp.bfloat16),
    ]
    if keys:
        scratch.append(pltpu.VMEM((64, count * depth), jnp.bfloat16))
    scratch.append(pltpu.SemaphoreType.DMA((count, 4)))
    return pl.pallas_call(
        functools.partial(project_kernel, count, keys, sums is None, end),
        out_shape=shapes,
        in_specs=[pl.BlockSpec(memory_space=pltpu.SMEM)]
        + [hbm] * (len(blocks) + len(weights))
        + [vmem] * len(sums or []),
        out_specs=[vmem] * len(shapes),
        scratch_shapes=scratch,
        compiler_params=pltpu.CompilerParams(vmem_limit_bytes=VMEM_BYTES),
        cost_estimate=QUICK,
        name="project",
    )(order, *blocks, *weights, *(sums or []))


def along_y(block):
    return [lax.ppermute(block, "head", route) for route in (Y_UP, Y_DOWN, Y_FAR)]


def pieces(dz, dc, own, others):
    return [(0, dz, dc, own)] * (own is not None) + [
        (dy, dz, dc, b) for dy, b in zip((3, 1, 2), others)
    ]


def exchange(pages):
    return lax.all_to_all(pages, "group", 0, 0, tiled=True)


def mark_kernel(numbers, chosen, hits, found):
    def page_step(k, carry):
        rows = pl.ds(pl.multiple_of(numbers[k], PAGE), WINDOW)
        slot = lax.broadcasted_iota(jnp.int32, (WINDOW, PAGE), 1) + k * PAGE
        hit = jnp.where(chosen[rows, :] == slot, 1.0, 0.0)
        hits[k] = hit.astype(jnp.bfloat16)
        found[k] = jnp.broadcast_to(jnp.max(hit, axis=0, keepdims=True), (8, PAGE))
        return carry

    lax.fori_loop(0, CTXP, page_step, 0)


def mark(numbers, chosen):
    vmem = pl.BlockSpec(memory_space=pltpu.VMEM)
    return pl.pallas_call(
        mark_kernel,
        out_shape=(
            jax.ShapeDtypeStruct((CTXP, WINDOW, PAGE), jnp.bfloat16),
            jax.ShapeDtypeStruct((CTXP, 8, PAGE), jnp.float32),
        ),
        in_specs=[pl.BlockSpec(memory_space=pltpu.SMEM), vmem],
        out_specs=(vmem, vmem),
        compiler_params=pltpu.CompilerParams(vmem_limit_bytes=32 * 1024 * 1024),
        cost_estimate=QUICK,
        name="mark",
    )(numbers, chosen)


def refresh_kernel(count, numbers, *refs):
    given = 6 if count > 1 else 1
    context, new = refs[:given], refs[given : given + count]
    hits, found, result, fresh = refs[given + count :]
    rank = numbers[40] if count > 1 else 0
    width = 32 * count
    places = [
        [pl.multiple_of(c * width + (rank ^ j) * 32, 32) for c in range(2)] for j in range(count)
    ]
    for j in range(count):
        for c in range(2):
            fresh[pl.ds(places[j][c], 32), :] = new[j][pl.ds(c * 32, 32), :]

    def page_step(k, carry, parts, before):
        rows = pl.ds(pl.multiple_of(numbers[k], PAGE), WINDOW)
        moved = jnp.dot(fresh[:, rows], hits[k], preferred_element_type=jnp.float32)
        taken = found[k, pl.ds(0, 1), :] > 0.0
        if count == 1:
            old = parts[0][k].reshape(2 * width, PAGE).astype(jnp.float32)
            now = jnp.where(taken, moved, old).astype(jnp.bfloat16)
            result[k] = now.reshape(2, width, PAGE)
            return carry
        lanes = pl.ds(pl.multiple_of(k * PAGE, PAGE), PAGE)
        for j in range(count):
            for c in range(2):
                page = k if j < 2 else k - before
                result[pl.ds(places[j][c], 32), lanes] = parts[j][page, c]
        old = result[:, lanes].astype(jnp.float32)
        result[:, lanes] = jnp.where(taken, moved, old).astype(jnp.bfloat16)
        return carry

    step = functools.partial(page_step, parts=context[:4], before=0)
    if count == 1:
        lax.fori_loop(0, CTXP, step, 0, unroll=4)
    else:
        lax.fori_loop(0, FIRST_PAGES, step, 0, unroll=4)
        step = functools.partial(
            page_step, parts=context[:2] + context[4:], before=FIRST_PAGES
        )
        lax.fori_loop(FIRST_PAGES, CTXP, step, 0, unroll=4)
        result[:, pl.ds(CTX, TXT)] = fresh[:, pl.ds(SEL, TXT)]


def attend_kernel(numbers, q, kv, first, last, attended):
    text_count = numbers[41]

    def fold(carry, scores, values):
        peak, total, mixed = carry
        new_peak = jnp.maximum(peak, jnp.max(scores, axis=1, keepdims=True))
        fade = jnp.exp2((peak - new_peak) * EXP2_SCALE)
        terms = jnp.exp2((scores - new_peak) * EXP2_SCALE)
        total = total * fade + jnp.sum(terms, axis=1, keepdims=True)
        mixed = mixed * fade + lax.dot_general(
            terms.astype(jnp.bfloat16),
            values,
            (((1,), (1,)), ((), ())),
            preferred_element_type=jnp.float32,
        )
        return new_peak, total, mixed

    for block in range(R // ROWS):
        rows = pl.ds(block * ROWS, ROWS)
        query = jnp.concatenate([q[rows, pl.ds(0, HD)], q[rows, pl.ds(HD, HD)]], axis=0)
        carry = (
            jnp.full((2 * ROWS, 1), LOW, jnp.float32),
            jnp.zeros((2 * ROWS, 1), jnp.float32),
            jnp.zeros((2 * ROWS, HD), jnp.float32),
        )
        image_rows = block < SEL // ROWS

        def image_step(k, carry, query=query, rows=rows, begin=numbers[32 + min(block, 3)]):
            wanted = begin + k * KEYS
            start = pl.multiple_of(jnp.minimum(wanted, CTX - KEYS), PAGE)
            lanes = pl.ds(start, KEYS)
            scores = jnp.dot(query, kv[pl.ds(0, HD), lanes], preferred_element_type=jnp.float32)
            slot = lax.broadcasted_iota(jnp.int32, (ROWS, KEYS), 1) + start
            low = jnp.maximum(first[rows, pl.ds(0, 1)], wanted)
            allowed = (slot >= low) & (slot <= last[rows, pl.ds(0, 1)])
            scores = jnp.where(jnp.concatenate([allowed, allowed], axis=0), scores, LOW)
            return fold(carry, scores, kv[pl.ds(HD, HD), lanes])

        if image_rows:
            carry = lax.fori_loop(0, numbers[36 + block], image_step, carry)
        else:
            for k in range(CTX // TEXT_KEYS):
                lanes = pl.ds(k * TEXT_KEYS, TEXT_KEYS)
                scores = jnp.dot(
                    query, kv[pl.ds(0, HD), lanes], preferred_element_type=jnp.float32
                )
                carry = fold(carry, scores, kv[pl.ds(HD, HD), lanes])
            lanes = pl.ds(CTX, TXT)
            scores = jnp.dot(query, kv[pl.ds(0, HD), lanes], preferred_element_type=jnp.float32)
            slot = lax.broadcasted_iota(jnp.int32, (TXT, TXT), 1)
            row = lax.broadcasted_iota(jnp.int32, (TXT, TXT), 0)
            allowed = (slot <= row) & (slot < text_count)
            scores = jnp.where(jnp.concatenate([allowed, allowed], axis=0), scores, LOW)
            carry = fold(carry, scores, kv[pl.ds(HD, HD), lanes])
        _, total, mixed = carry
        mixed = (mixed / total).astype(jnp.bfloat16)
        attended[rows, pl.ds(0, HD)] = mixed[:ROWS]
        attended[rows, pl.ds(HD, HD)] = mixed[ROWS:]


def refresh(numbers, context, fresh, marks):
    vmem = pl.BlockSpec(memory_space=pltpu.VMEM)
    count = len(fresh)
    shape = (2 * HD, CTX + TXT) if count > 1 else (CTXP, 2, 32, PAGE)
    return pl.pallas_call(
        functools.partial(refresh_kernel, count),
        out_shape=jax.ShapeDtypeStruct(shape, jnp.bfloat16),
        in_specs=[pl.BlockSpec(memory_space=pltpu.SMEM)] + [vmem] * (len(context) + count + 2),
        out_specs=vmem,
        scratch_shapes=[pltpu.VMEM((64 * count, R), jnp.bfloat16)],
        compiler_params=pltpu.CompilerParams(vmem_limit_bytes=32 * 1024 * 1024),
        cost_estimate=QUICK,
        name="refresh",
    )(numbers, *context, *fresh, *marks)


def attend(numbers, q, kv, first, last):
    vmem = pl.BlockSpec(memory_space=pltpu.VMEM)
    return pl.pallas_call(
        attend_kernel,
        out_shape=jax.ShapeDtypeStruct((R, 2 * HD), jnp.bfloat16),
        in_specs=[pl.BlockSpec(memory_space=pltpu.SMEM)] + [vmem] * 4,
        out_specs=vmem,
        compiler_params=pltpu.CompilerParams(vmem_limit_bytes=32 * 1024 * 1024),
        cost_estimate=QUICK,
        name="attend",
    )(numbers, q, kv, first, last)


def replace_kernel(places, pool, pages, out):
    out[...] = pool[...]

    def step(i, carry):
        place = places[i]

        @pl.when(place < POOL_DEV)
        def _():
            out[jnp.minimum(place, POOL_DEV - 1)] = pages[i]

        return carry

    lax.fori_loop(0, places.shape[0], step, 0)


def replace(places, pool, pages):
    vmem = pl.BlockSpec(memory_space=pltpu.VMEM)
    return pl.pallas_call(
        replace_kernel,
        out_shape=jax.ShapeDtypeStruct(pool.shape, pool.dtype),
        in_specs=[pl.BlockSpec(memory_space=pltpu.SMEM), vmem, vmem],
        out_specs=vmem,
        compiler_params=pltpu.CompilerParams(vmem_limit_bytes=16 * 1024 * 1024),
        cost_estimate=QUICK,
        name="replace",
    )(places, pool, pages)


def slot_numbers(owners):
    entries = owners.shape[-1]
    earlier = jnp.arange(entries)[None, :] < jnp.arange(entries)[:, None]
    same_owner = owners[..., None, :] == owners[..., :, None]
    return jnp.sum(same_owner & earlier, axis=-1)


def body(
    rows_in, w_query, w_key, w_value, w_out, kv_pool, page_table, image_pages, selected, text_len
):
    group_index = lax.axis_index("group")
    head_index = lax.axis_index("head")
    place = (head_index // 4, head_index // 2 % 2, head_index % 2)
    capacity = 2 * CTXP // lax.axis_size("group")
    page_shape = kv_pool.shape[1:]

    far = swap_z(rows_in)
    near = along_y(rows_in)
    near_core, page_table = meet(swap_core(rows_in), page_table)

    owners = page_table // POOL_DEV
    local_page = page_table % POOL_DEV
    slot_of = slot_numbers(owners)
    held_here = (owners == group_index)[:, :, None] & (
        slot_of[:, :, None] == jnp.arange(capacity)[None, None, :]
    )
    held_place = jnp.sum(jnp.where(held_here, local_page[:, :, None], 0), axis=1)
    held_valid = jnp.any(held_here, axis=1)
    my_owners = lax.dynamic_index_in_dim(owners, group_index, 0, keepdims=False)
    my_slots = lax.dynamic_index_in_dim(slot_of, group_index, 0, keepdims=False)
    pages = kv_pool[held_place]
    near[0], near[1], far, pages = meet(near[0], near[1], far, pages)
    pages = exchange(pages)
    near_cores = [swap_core(b) for b in near]
    far, near_core, *near_cores = meet(far, near_core, *near_cores)

    far_core = swap_core(far)
    fars = along_y(far)
    weights = (w_query, w_key.T, w_value.T)
    blocks = pieces(0, 0, rows_in, near) + pieces(0, 1, near_core, near_cores)
    blocks += pieces(1, 0, far, []) + pieces(1, 1, far_core, [])
    sums = project(blocks, weights, place, None, False)
    positions = selected[0]
    image_ends = jnp.cumsum(image_pages[0]) * PAGE
    image_first = jnp.max(
        jnp.where(positions[:, None] >= image_ends[None, :], image_ends[None, :], 0), axis=1
    )
    page_first = jnp.sum(positions[None, :] < (jnp.arange(CTXP) * PAGE)[:, None], axis=1)
    window = jnp.minimum(page_first // PAGE * PAGE, SEL - WINDOW)
    key_first = image_first[::ROWS]
    key_steps = (positions[ROWS - 1 :: ROWS] - key_first) // KEYS + 1
    numbers = jnp.concatenate(
        [window, key_first, key_steps, (head_index % 4)[None], text_len]
    ).astype(jnp.int32)
    wide = lambda v: jnp.broadcast_to(v[:, None], (SEL, 128)).astype(jnp.int32)
    wide_positions, wide_first = wide(positions), wide(image_first)
    target = (my_owners == jnp.arange(16)[:, None])[:, None, :] & (
        my_slots == jnp.arange(capacity)[:, None]
    )
    back_index = jnp.sum(jnp.where(target, jnp.arange(CTXP), 0), axis=2)
    marks = mark(numbers, wide_positions)

    values = meet(pages, *sums, *marks, numbers, wide_first, back_index, my_owners, my_slots)
    pages, sums, marks = values[0], values[1:3], values[3:5]
    numbers, wide_first, back_index, my_owners, my_slots = values[5:]
    own_context = pages[my_owners, my_slots]
    z_first = swap_z(own_context[:FIRST_PAGES])
    z_rest = swap_z(own_context[FIRST_PAGES:])
    core_context = swap_core(own_context)
    z_first, *fars = meet(z_first, *fars)
    far_cores = [swap_core(b) for b in fars]
    z_first_core = swap_core(z_first)
    core_context, *sums = meet(core_context, *sums)
    blocks = pieces(1, 0, None, fars) + pieces(1, 1, None, far_cores)
    queries, new_kv = project(blocks, weights, place, sums, True)
    z_kv = swap_z(new_kv)
    core_kv = swap_core(new_kv)

    returned = refresh(numbers, [own_context], [new_kv], marks)
    homeward = returned[back_index]
    z_kv, core_kv, homeward, z_rest = meet(z_kv, core_kv, homeward, z_rest)
    arrived = exchange(homeward)

    context = [own_context, core_context, z_first, z_first_core, z_rest, swap_core(z_rest)]
    fresh = [new_kv, core_kv, z_kv, swap_core(z_kv)]
    kv = refresh(numbers, context, fresh, marks)
    attended = attend(numbers, queries, kv, wide_first, wide_positions)

    far = swap_z(attended)
    near = along_y(attended)
    near_core = swap_core(attended)
    near_cores = [swap_core(b) for b in near]
    far, near_core, *near_cores = meet(far, near_core, *near_cores)

    far_core = swap_core(far)
    fars = along_y(far)
    blocks = pieces(0, 0, attended, near) + pieces(0, 1, near_core, near_cores)
    blocks += pieces(1, 0, far, []) + pieces(1, 1, far_core, [])
    sums = project(blocks, (w_out,), place, None, False)
    places = jnp.where(held_valid, held_place, POOL_DEV).reshape(16 * capacity)
    new_pool = replace(
        places.astype(jnp.int32), kv_pool, arrived.reshape(16 * capacity, *page_shape)
    )
    values = meet(*fars, new_pool, *sums)
    fars, new_pool, sums = values[:3], values[3], values[4:]
    far_cores = [swap_core(b) for b in fars]
    blocks = pieces(1, 0, None, fars) + pieces(1, 1, None, far_cores)
    (out,) = project(blocks, (w_out,), place, sums, True)
    return (out, new_pool)


def solution(mesh):
    placed = (
        P("group", "head"),
        P(None, "head"),
        P(None, "head"),
        P(None, "head"),
        P(None, "head"),
        P("group", None, "head", None),
        P(),
        P("group", None),
        P("group", None),
        P("group"),
    )
    return jax.shard_map(
        body,
        mesh=mesh,
        in_specs=placed,
        out_specs=(P("group", "head"), P("group", None, "head", None)),
        check_vma=False,
    )
```
